512 devices in a mesh: image: 8 (over x, core), slab: 64 (over z, y).
Axes of the slice: x: 4, y: 8, z: 8, core: 2. Of those that a mesh axis runs over, the one named last changes fastest.
Arguments:
- string: float32 [16, 2048, 4096], P('image', 'slab'), may hold values from -1.2 to 1.2
- tilt: float32 [2048, 4096], P('slab'), may hold values from -0.5 to 0.5
- source_pair: int32 [16], replicated, may hold values from 0 to 14, as said below
Outputs:
- new_string: float32 [16, 2048, 4096], P('image', 'slab')
The draws below stay inside these ranges and needn't reach their ends.
Inputs may be any that keep to these rules, and one draw needn't show every extreme that they name: source_pair[j] lies between j - 2 and j; the first entry is 0 and the last is 14.
All inputs are finite; a program needn't handle non-finite values.
Results may differ from the reference program's by a relative error of at most 0.00012.
Values sent between devices are 32-bit elements; how exact they have to be, the bound alone decides.
No kernel may reach another device: no remote copies, remote signals or barrier semaphores. Data moves between devices by JAX's collectives and lax.ppermute only.
A program may use at most 64 MiB of HBM per device.

```python
import jax
import jax.numpy as jnp
from jax import lax

GX = 4096
SUBSTEPS = 8
IMAGES = 16
NY = 2048


def draw_source_pair(key, part):
    key = jax.random.fold_in(key, 7)
    index = jnp.arange(IMAGES, dtype=jnp.int32)
    offset = jax.random.randint(key, (IMAGES,), -2, 1, dtype=jnp.int32)
    lower = jnp.clip(index + offset, 0, IMAGES - 2)
    lower = lower.at[0].set(0)
    lower = lower.at[IMAGES - 1].set(IMAGES - 2)
    return lower.astype(jnp.int32)


def shard_levels(own_key, dims, pieces, smallest, largest):
    def one(axis_at, shards_of):
        draws = jax.random.uniform(jax.random.fold_in(jax.random.fold_in(own_key, 6), axis_at), (shards_of,), jnp.float32, smallest / len(pieces), largest / len(pieces))
        return jnp.repeat(jnp.exp(draws), dims[axis_at] // shards_of).reshape((-1,) + (1,) * (len(dims) - axis_at - 1))

    loudness = one(*pieces[0])
    for cut in pieces[1:]:
        loudness = loudness * one(*cut)
    return loudness


def setup_inputs(seed: int = 0) -> dict:
    arg_keys = jax.random.split(jax.random.key(seed), 4)
    return {
        "string": jnp.clip(jax.random.uniform(arg_keys[0], (IMAGES, NY, GX), jnp.float32, -1.2, 1.2) * shard_levels(arg_keys[0], (IMAGES, NY, GX), ((0, 8), (1, 64)), -0.4, 0.0), -1.2, 1.2),
        "tilt": jnp.clip(jax.random.uniform(arg_keys[1], (NY, GX), jnp.float32, -0.5, 0.5) * shard_levels(arg_keys[1], (NY, GX), ((0, 64),), -0.4, 0.0), -0.5, 0.5),
        "source_pair": draw_source_pair(jax.random.fold_in(arg_keys[3], 71), 0),
    }


DT = 0.1
EPS = 1e-06

def flow_step(field, tilt):
    lap = jnp.roll(field, 1, 1) + jnp.roll(field, -1, 1) + jnp.roll(field, 1, 2) + jnp.roll(field, -1, 2) - 4.0 * field
    return field + DT * (lap + field - field * field * field + tilt[None])

def reference(string, tilt, source_pair):
    flowed = string
    for step in range(SUBSTEPS):
        flowed = flow_step(flowed, tilt)
    count = flowed.shape[0]
    cells = flowed.shape[1] * flowed.shape[2]
    diffs = flowed[1:] - flowed[:-1]
    squares = lax.optimization_barrier(jnp.sum(diffs * diffs, axis=(1, 2)))
    seg = jnp.sqrt(squares / cells + EPS)
    seg = jnp.concatenate([seg, jnp.zeros((1,), jnp.float32)])
    arc = jnp.concatenate([jnp.zeros((1,), jnp.float32), jnp.cumsum(seg[:-1])])
    total = arc[count - 1]
    targets = jnp.arange(count, dtype=jnp.int32).astype(jnp.float32) / (count - 1)
    weight = (targets * total - arc[source_pair]) / seg[source_pair]
    lower = jnp.take(flowed, source_pair, axis=0)
    upper = jnp.take(flowed, source_pair + 1, axis=0)
    weight = weight[:, None, None]
    return (1.0 - weight) * lower + weight * upper
```

```python
import functools

import jax
import jax.numpy as jnp
from jax import lax
from jax.experimental import pallas as pl
from jax.experimental.pallas import tpu as pltpu
from jax.sharding import PartitionSpec as P

SUBSTEPS = 8
DT = 0.1
EPS = 1e-06
LANES = 128
ROWS = 8
CHUNK = 8
VMEM_LIMIT = 48 * 1024 * 1024


def ring(axis, distance):
    count = lax.axis_size(axis)
    return [(i, (i + distance) % count) for i in range(count)]


def line(axis, distance):
    devices = range(lax.axis_size(axis))
    return [(i, i + distance) for i in devices if i + distance in devices]


def substep(source, target, tilt, row, blocks):
    lane = lax.broadcasted_iota(jnp.int32, (ROWS, LANES), 1)
    is_first = lane == 0
    is_last = lane == LANES - 1
    columns = blocks

    def chunk(index, carry):
        base = index * CHUNK
        places = [
            lax.rem(base + (j - 1 + columns), columns) if j in (0, CHUNK + 1) else base + (j - 1)
            for j in range(CHUNK + 2)
        ]
        forces = [tilt[places[j], pl.ds(row, ROWS), :] for j in range(1, CHUNK + 1)]
        for image in range(2):
            middle = [source[image, place, pl.ds(row, ROWS), :] for place in places]
            right_moved = [pltpu.roll(m, 1, 1) for m in middle[:-1]]
            left_moved = [pltpu.roll(m, LANES - 1, 1) for m in middle[1:]]
            for j in range(1, CHUNK + 1):
                u = middle[j]
                left = jnp.where(is_first, right_moved[j - 1], right_moved[j])
                right = jnp.where(is_last, left_moved[j], left_moved[j - 1])
                above = source[image, places[j], pl.ds(row - 1, ROWS), :]
                below = source[image, places[j], pl.ds(row + 1, ROWS), :]
                near = (above + below) + (left + right)
                target[image, places[j], pl.ds(row, ROWS), :] = (
                    u * (0.7 - DT * (u * u)) + (DT * near + forces[j - 1])
                )
        return carry

    lax.fori_loop(0, columns // CHUNK, chunk, 0)


def flow_kernel(string, tilt, low, high, first, second, even, odd, force):
    depth = string.shape[1]
    columns = string.shape[2] // LANES
    extended = depth + 2 * ROWS

    def load(c, carry):
        place = pl.ds(pl.multiple_of(c * LANES, LANES), LANES)
        for image in range(2):
            even[image, c, pl.ds(0, ROWS), :] = low[image, :, place]
            even[image, c, pl.ds(ROWS, depth), :] = string[image, :, place]
            even[image, c, pl.ds(ROWS + depth, ROWS), :] = high[image, :, place]
        force[c, pl.ds(0, ROWS), :] = DT * low[2, :, place]
        force[c, pl.ds(ROWS, depth), :] = DT * tilt[:, place]
        force[c, pl.ds(ROWS + depth, ROWS), :] = DT * high[2, :, place]
        return carry

    lax.fori_loop(0, columns, load, 0)
    buffers = (even, odd)
    for step in range(1, SUBSTEPS + 1):
        source, target = buffers[(step - 1) % 2], buffers[step % 2]
        last = extended - step - ROWS
        starts = sorted(set(list(range(step, last, ROWS)) + [last]))
        for row in starts:
            substep(source, target, force, row, columns)
    done = buffers[SUBSTEPS % 2]

    def store(c, carry):
        first[c] = done[0, c, pl.ds(ROWS, depth), :]
        second[c] = done[1, c, pl.ds(ROWS, depth), :]
        return carry

    lax.fori_loop(0, columns, store, 0)


def square_kernel(first, second, lower, out):
    columns = first.shape[0]
    shape = first.shape[1:]

    def one(c, sums):
        before = first[c] - lower[c]
        after = second[c] - first[c]
        return sums[0] + before * before, sums[1] + after * after

    zero = jnp.zeros(shape, jnp.float32)
    before, after = lax.fori_loop(0, columns, one, (zero, zero), unroll=4)
    before = jnp.sum(before, axis=(0, 1), keepdims=True)
    after = jnp.sum(after, axis=(0, 1), keepdims=True)
    lane = lax.broadcasted_iota(jnp.int32, (1, LANES), 1)
    row = jnp.where(lane == 0, before, jnp.where(lane == 1, after, 0.0))
    out[...] = jnp.broadcast_to(row[None], out.shape)


def total_kernel(parts, out):
    out[...] = jnp.broadcast_to(jnp.sum(parts[...], axis=0, keepdims=True), out.shape)


def mix_kernel(cells, images, rank, sources, squares, low_2, low_1, own_0, own_1, high_1, out):
    columns = own_0.shape[0]
    rows = squares.shape[0]
    squares = squares[...].reshape(rows, LANES)
    lane = lax.broadcasted_iota(jnp.int32, (rows, LANES), 1)
    index = 2 * lax.broadcasted_iota(jnp.int32, (rows, LANES), 0) - 1 + lane
    used = (lane < 2) & (index >= 0) & (index < images - 1)
    seg = jnp.where(used, jnp.sqrt(squares / cells + EPS), 0.0)
    total = jnp.sum(seg, axis=(0, 1), keepdims=True)
    first = 2 * rank[0]
    shares = []
    for t in range(2):
        target = first + t
        source = sources[target]
        arc = jnp.sum(jnp.where(index < source, seg, 0.0), axis=(0, 1), keepdims=True)
        length = jnp.sum(jnp.where(index == source, seg, 0.0), axis=(0, 1), keepdims=True)
        ratio = target.astype(jnp.float32) / (images - 1)
        weight = (ratio * total - arc) / length
        place = source - (first - 2)
        shares.append(
            [
                jnp.where(place == m, 1.0 - weight, 0.0) + jnp.where(place + 1 == m, weight, 0.0)
                for m in range(5)
            ]
        )

    def one(c, carry):
        fields = [ref[c] for ref in (low_2, low_1, own_0, own_1, high_1)]
        place = pl.ds(pl.multiple_of(c * LANES, LANES), LANES)
        for t in range(2):
            result = shares[t][0] * fields[0]
            for m in range(1, 5):
                result = result + shares[t][m] * fields[m]
            out[t, :, place] = result
        return carry

    lax.fori_loop(0, columns, one, 0)


def call(kernel, shapes, count, scratch=(), smem=0):
    vmem = pl.BlockSpec(memory_space=pltpu.VMEM)
    return pl.pallas_call(
        kernel,
        out_shape=shapes,
        in_specs=[pl.BlockSpec(memory_space=pltpu.SMEM)] * smem + [vmem] * count,
        out_specs=jax.tree.map(lambda _: vmem, shapes),
        scratch_shapes=list(scratch),
        compiler_params=pltpu.CompilerParams(vmem_limit_bytes=VMEM_LIMIT),
    )


def body(string, tilt, source_pair):
    count, depth, width = string.shape
    columns = width // LANES
    slabs = lax.axis_size("slab")
    ranks = lax.axis_size("image")
    up = jnp.concatenate([string[:, depth - ROWS :], tilt[None, depth - ROWS :]], axis=0)
    down = jnp.concatenate([string[:, :ROWS], tilt[None, :ROWS]], axis=0)
    low = lax.ppermute(up, "slab", ring("slab", 1))
    high = lax.ppermute(down, "slab", ring("slab", -1))
    field = jax.ShapeDtypeStruct((columns, depth, LANES), jnp.float32)
    extended = depth + 2 * ROWS
    first, second = call(
        flow_kernel,
        (field, field),
        4,
        [
            pltpu.VMEM((2, columns, extended, LANES), jnp.float32),
            pltpu.VMEM((2, columns, extended, LANES), jnp.float32),
            pltpu.VMEM((columns, extended, LANES), jnp.float32),
        ],
    )(string, tilt, low, high)
    low_1 = lax.ppermute(second, "image", line("image", 1))
    high_1 = lax.ppermute(first, "image", line("image", -1))
    low_2 = lax.ppermute(first, "image", line("image", 1))
    parts = call(square_kernel, jax.ShapeDtypeStruct((slabs, 1, LANES), jnp.float32), 3)(
        first, second, low_1
    )
    parts = lax.all_to_all(parts, "slab", 0, 0)
    sums = call(total_kernel, jax.ShapeDtypeStruct((ranks, 1, LANES), jnp.float32), 1)(parts)
    sums = lax.all_to_all(sums, "image", 0, 0)
    rank = lax.axis_index("image").reshape(1)
    cells = depth * slabs * width
    return call(
        functools.partial(mix_kernel, cells, count * ranks),
        jax.ShapeDtypeStruct(string.shape, jnp.float32),
        6,
        smem=2,
    )(rank, source_pair, sums, low_2, low_1, first, second, high_1)


def solution(mesh):
    placed = (P("image", "slab", None), P("slab", None), P())
    return jax.shard_map(
        body, mesh=mesh, in_specs=placed, out_specs=P("image", "slab", None), check_vma=False
    )
```

```python
import functools

import jax
import jax.numpy as jnp
from jax import lax
from jax.experimental import pallas as pl
from jax.experimental.pallas import tpu as pltpu
from jax.sharding import PartitionSpec as P

SUBSTEPS = 8
DT = 0.1
EPS = 1e-06
LANES = 128
ROWS = 8
VMEM_LIMIT = 48 * 1024 * 1024
HALO_LIMIT = 54136 * 1024


def ring(axis, distance):
    count = lax.axis_size(axis)
    return [(i, (i + distance) % count) for i in range(count)]


def line(axis, distance):
    devices = range(lax.axis_size(axis))
    return [(i, i + distance) for i in devices if i + distance in devices]


def substep(source, target, force, row, out_row, force_row, columns):
    lane = lax.broadcasted_iota(jnp.int32, (ROWS, LANES), 1)
    is_first = lane == 0
    is_last = lane == LANES - 1
    middle = [source[c % columns, pl.ds(row, ROWS), :] for c in range(-1, columns + 1)]
    right_moved = [pltpu.roll(m, 1, 1) for m in middle[:-1]]
    left_moved = [pltpu.roll(m, LANES - 1, 1) for m in middle[1:]]
    for c in range(columns):
        u = middle[c + 1]
        left = jnp.where(is_first, right_moved[c], right_moved[c + 1])
        right = jnp.where(is_last, left_moved[c + 1], left_moved[c])
        above = source[c, pl.ds(row - 1, ROWS), :]
        below = source[c, pl.ds(row + 1, ROWS), :]
        near = (above + below) + (left + right)
        target[c, pl.ds(out_row, ROWS), :] = u * (0.7 - DT * (u * u)) + (
            DT * near + force[c, pl.ds(force_row, ROWS), :]
        )


def halo_kernel(string, tilt, up, down, sems):
    depth = string.shape[1]
    copies = [
        pltpu.make_async_copy(string.at[:, pl.ds(depth - ROWS, ROWS)], up.at[pl.ds(0, 2)], sems.at[0]),
        pltpu.make_async_copy(tilt.at[pl.ds(depth - ROWS, ROWS)], up.at[2], sems.at[1]),
        pltpu.make_async_copy(string.at[:, pl.ds(0, ROWS)], down.at[pl.ds(0, 2)], sems.at[2]),
        pltpu.make_async_copy(tilt.at[pl.ds(0, ROWS)], down.at[2], sems.at[3]),
    ]
    for copy in copies:
        copy.start()
    for copy in copies:
        copy.wait()


def plan_weights(images, rank, sources, plan):
    shape = plan.shape[2:]
    lane = lax.broadcasted_iota(jnp.int32, shape, 1)
    index = 2 * lax.broadcasted_iota(jnp.int32, shape, 0) + lane
    used = (lane < 2) & (index < images - 1)
    first = 2 * rank[0]
    for t in range(2):
        target = first + t
        source = sources[target]
        place = source - (first - 2)
        plan[t, 0] = jnp.where(used & (index < source), 1.0, 0.0)
        plan[t, 1] = jnp.where(used & (index == source), 1.0, 0.0)
        plan[t, 2] = jnp.full(shape, target.astype(jnp.float32) / (images - 1))
        for m in range(5):
            plan[t, 3 + m] = jnp.full(shape, jnp.where(place == m, 1.0, 0.0))
            plan[t, 8 + m] = jnp.full(shape, jnp.where(place + 1 == m, 1.0, 0.0))


def inner_kernel(images, rank, sources, string, tilt, plan, full, mid_first, history, edge_force, even, odd, force):
    plan_weights(images, rank, sources, plan)
    depth = string.shape[1]
    columns = string.shape[2] // LANES
    for c in range(columns):
        place = pl.ds(c * LANES, LANES)
        for image in range(2):
            even[image, c] = string[image, :, place]
        scaled = DT * tilt[:, place]
        force[c] = scaled
        edge_force[c, pl.ds(0, ROWS), :] = scaled[:ROWS]
        edge_force[c, pl.ds(ROWS, ROWS), :] = scaled[depth - ROWS :]
    buffers = (even, odd)
    for step in range(1, SUBSTEPS + 1):
        source, target = buffers[(step - 1) % 2], buffers[step % 2]
        last = depth - step - ROWS
        for image in range(2):
            for c in range(columns):
                history[0, image, c, pl.ds(2 * step - 2, 2), :] = source[image, c, pl.ds(step - 1, 2), :]
                history[1, image, c, pl.ds(2 * step - 2, 2), :] = source[
                    image, c, pl.ds(depth - 1 - step, 2), :
                ]
            for row in sorted(set(list(range(step, last, ROWS)) + [last])):
                if step < SUBSTEPS:
                    substep(source.at[image], target.at[image], force, row, row, row, columns)
                else:
                    substep(source.at[image], full.at[image], force, row, row, row, columns)
    mid_first[...] = full[0, :, pl.ds(ROWS, depth - 2 * ROWS), :]


def edge_kernel(low, high, history, edge_force, inner, full, edge_first, top_even, top_odd, bottom_even, bottom_odd, force):
    columns, depth = full.shape[1:3]
    for c in range(columns):
        place = pl.ds(c * LANES, LANES)
        for image in range(2):
            top_even[image, c, pl.ds(0, ROWS), :] = low[image, :, place]
            bottom_even[image, c, pl.ds(ROWS, ROWS), :] = high[image, :, place]
        force[0, c, pl.ds(0, ROWS), :] = DT * low[2, :, place]
        force[0, c, pl.ds(ROWS, ROWS), :] = edge_force[c, pl.ds(0, ROWS), :]
        force[1, c, pl.ds(0, ROWS), :] = edge_force[c, pl.ds(ROWS, ROWS), :]
        force[1, c, pl.ds(ROWS, ROWS), :] = DT * high[2, :, place]
    tops, bottoms = (top_even, top_odd), (bottom_even, bottom_odd)
    for step in range(1, SUBSTEPS + 1):
        now, later = (step - 1) % 2, step % 2
        for image in range(2):
            top, bottom = tops[now].at[image], bottoms[now].at[image]
            for c in range(columns):
                top[c, pl.ds(ROWS, 2), :] = history[0, image, c, pl.ds(2 * step - 2, 2), :]
                bottom[c, pl.ds(ROWS - 2, 2), :] = history[1, image, c, pl.ds(2 * step - 2, 2), :]
            top_out, bottom_out = tops[later].at[image], bottoms[later].at[image]
            bottom_row = ROWS
            if step == SUBSTEPS:
                top_out = bottom_out = full.at[image]
                bottom_row = depth - ROWS
            substep(top, top_out, force.at[0], 1, 0, step, columns)
            substep(bottom, bottom_out, force.at[1], ROWS - 1, bottom_row, ROWS - step, columns)
    edge_first[:, pl.ds(0, ROWS), :] = full[0, :, pl.ds(0, ROWS), :]
    edge_first[:, pl.ds(ROWS, ROWS), :] = full[0, :, pl.ds(depth - ROWS, ROWS), :]


def differences(upper, lower, columns, sums):
    def one(c, total):
        difference = upper(c) - lower(c)
        return total + difference * difference

    return lax.fori_loop(0, columns, one, sums, unroll=8)


def local_kernel(full, mid_high, sums):
    columns, depth = full.shape[1:3]
    zero = jnp.zeros((depth, LANES), jnp.float32)
    sums[0] = differences(lambda c: full[1, c], lambda c: full[0, c], columns, zero)
    middle = pl.ds(ROWS, depth - 2 * ROWS)
    sums[1] = jnp.zeros((depth, LANES), jnp.float32)
    sums[1, middle, :] = differences(lambda c: mid_high[c], lambda c: full[1, c, middle], columns, zero[: depth - 2 * ROWS])


def square_kernel(sums, full, edge_high, out):
    columns, depth = full.shape[1:3]
    beyond = jnp.sum(sums[1].reshape(-1, ROWS, LANES), axis=0)
    for row, out_row in ((0, 0), (ROWS, depth - ROWS)):
        beyond = differences(
            lambda c: edge_high[c, pl.ds(row, ROWS)], lambda c: full[1, c, pl.ds(out_row, ROWS)], columns, beyond
        )
    after = jnp.sum(sums[0], axis=(0, 1), keepdims=True)
    beyond = jnp.sum(beyond, axis=(0, 1), keepdims=True)
    lane = lax.broadcasted_iota(jnp.int32, (1, LANES), 1)
    row = jnp.where(lane == 0, after, jnp.where(lane == 1, beyond, 0.0))
    out[...] = jnp.broadcast_to(row[None], out.shape)


def total_kernel(parts, full_low, out):
    out[...] = jnp.broadcast_to(jnp.sum(parts[...], axis=0, keepdims=True), out.shape)


def mix_kernel(cells, images, squares, plan, full, full_low, mid_high, edge_high, out, mixed, sems):
    columns, depth = full.shape[1:3]
    rows = squares.shape[0]
    seg = jnp.sqrt(squares[...].reshape(rows, LANES) / cells + EPS)
    lane = lax.broadcasted_iota(jnp.int32, (rows, LANES), 1)
    index = 2 * lax.broadcasted_iota(jnp.int32, (rows, LANES), 0) + lane
    seg = jnp.where((lane < 2) & (index < images - 1), seg, 0.0)

    def whole(values):
        return jnp.sum(values, axis=(0, 1), keepdims=True)

    total = whole(seg)
    shares = []
    for t in range(2):
        ratio = plan[t, 2]
        weight = (ratio * total - whole(plan[t, 0] * seg)) / whole(plan[t, 1] * seg)
        shares.append([(1.0 - weight) * plan[t, 3 + m] + weight * plan[t, 8 + m] for m in range(5)])
    group = columns // 4
    copies = []
    for g in range(4):
        for c in range(g * group, (g + 1) * group):
            place = pl.ds(c * LANES, LANES)
            for high, row, out_row in (
                (edge_high, 0, 0),
                (mid_high, 0, ROWS),
                (mid_high, ROWS, 2 * ROWS),
                (edge_high, ROWS, depth - ROWS),
            ):
                at = pl.ds(out_row, ROWS)
                fields = [full_low[0, c, at], full_low[1, c, at], full[0, c, at], full[1, c, at]]
                fields.append(high[c, pl.ds(row, ROWS)])
                for t in range(2):
                    result = shares[t][0] * fields[0]
                    for m in range(1, 5):
                        result = result + shares[t][m] * fields[m]
                    mixed[t, at, place] = result
        span = pl.ds(g * group * LANES, group * LANES)
        copy = pltpu.make_async_copy(mixed.at[:, :, span], out.at[:, :, span], sems.at[g])
        copy.start()
        copies.append(copy)
    for copy in copies:
        copy.wait()


VMEM = pl.BlockSpec(memory_space=pltpu.VMEM)
SMEM = pl.BlockSpec(memory_space=pltpu.SMEM)
HBM = pl.BlockSpec(memory_space=pltpu.HBM)
ANY = pl.BlockSpec(memory_space=pl.ANY)


def call(name, kernel, shapes, ins, scratch=(), outs=VMEM, cost=0, limit=VMEM_LIMIT, aliases=None):
    return pl.pallas_call(
        kernel,
        out_shape=shapes,
        in_specs=ins,
        out_specs=jax.tree.map(lambda _: outs, shapes),
        scratch_shapes=list(scratch),
        name=name,
        input_output_aliases=aliases or {},
        cost_estimate=pl.CostEstimate(flops=cost, bytes_accessed=1 << 20, transcendentals=0),
        compiler_params=pltpu.CompilerParams(vmem_limit_bytes=limit),
    )


def body(string, tilt, source_pair):
    count, depth, width = string.shape
    columns = width // LANES
    slabs = lax.axis_size("slab")
    ranks = lax.axis_size("image")
    images = count * ranks
    half = 2 * ROWS

    def array(*shape):
        return jax.ShapeDtypeStruct(shape, jnp.float32)

    def room(*shape):
        return pltpu.VMEM(shape, jnp.float32)

    halo = array(3, ROWS, width)
    up, down = call(
        "halo", halo_kernel, (halo, halo), [HBM] * 2, [pltpu.SemaphoreType.DMA((4,))], limit=HALO_LIMIT
    )(string, tilt)
    low = lax.ppermute(up, "slab", ring("slab", 1))
    high = lax.ppermute(down, "slab", ring("slab", -1))
    whole = array(2, columns, depth, LANES)
    single = array(columns, half, LANES)
    rank = lax.axis_index("image").reshape(1)
    plan, full, mid_first, history, edge_force = call(
        "inner",
        functools.partial(inner_kernel, images),
        (array(2, 13, ranks, LANES), whole, single, array(2, 2, columns, half, LANES), single),
        [SMEM] * 2 + [VMEM] * 2,
        [room(2, columns, depth, LANES), room(2, columns, depth, LANES), room(columns, depth, LANES)],
        cost=1 << 32,
    )(rank, source_pair, string, tilt)
    mid_high = lax.ppermute(mid_first, "image", line("image", -1))
    full, edge_first = call(
        "edge",
        edge_kernel,
        (whole, single),
        [VMEM] * 5,
        [room(2, columns, half, LANES)] * 4 + [room(2, columns, half, LANES)],
        cost=1 << 31,
        aliases={4: 0},
    )(low, high, history, edge_force, full)
    edge_high = lax.ppermute(edge_first, "image", line("image", -1))
    full_low = lax.ppermute(full, "image", line("image", 1))
    sums = call("local", local_kernel, array(2, depth, LANES), [VMEM] * 2, cost=1 << 28)(full, mid_high)
    parts = call("square", square_kernel, array(slabs, 1, LANES), [VMEM] * 3, cost=1 << 33)(sums, full, edge_high)
    parts = lax.all_to_all(parts, "slab", 0, 0)
    squares = call("total", total_kernel, array(ranks, 1, LANES), [VMEM, ANY], cost=1 << 33)(parts, full_low)
    squares = lax.all_to_all(squares, "image", 0, 0)
    cells = depth * slabs * width
    return call(
        "mix",
        functools.partial(mix_kernel, cells, images),
        array(*string.shape),
        [VMEM] * 6,
        [room(*string.shape), pltpu.SemaphoreType.DMA((4,))],
        outs=ANY,
    )(squares, plan, full, full_low, mid_high, edge_high)


def solution(mesh):
    placed = (P("image", "slab", None), P("slab", None), P())
    return jax.shard_map(
        body, mesh=mesh, in_specs=placed, out_specs=P("image", "slab", None), check_vma=False
    )
```

```python
import functools

import jax
import jax.numpy as jnp
from jax import lax
from jax.experimental import pallas as pl
from jax.experimental.pallas import tpu as pltpu
from jax.sharding import PartitionSpec as P

SUBSTEPS = 8
DT = 0.1
EPS = 1e-06
LANES = 128
ROWS = 8
VMEM_LIMIT = 48 * 1024 * 1024
HALO_LIMIT = 54136 * 1024


def partners(axis, first):
    count = lax.axis_size(axis)
    step = 1 if first else -1
    evens = range(0, count, 2)
    return [(i, (i + step) % count) for i in evens] + [((i + step) % count, i) for i in evens]


def line(axis, distance):
    devices = range(lax.axis_size(axis))
    return [(i, i + distance) for i in devices if i + distance in devices]


def is_odd(axis):
    return lax.rem(lax.axis_index(axis), 2)


def odd_mask():
    return jnp.full((ROWS, LANES), is_odd("slab"), jnp.int32) == 1


def substep(source, target, force, row, out_row, force_row, columns, keep=None, keep_row=0):
    lane = lax.broadcasted_iota(jnp.int32, (ROWS, LANES), 1)
    is_first = lane == 0
    is_last = lane == LANES - 1
    middle = [source[c % columns, pl.ds(row, ROWS), :] for c in range(-1, columns + 1)]
    right_moved = [pltpu.roll(m, 1, 1) for m in middle[:-1]]
    left_moved = [pltpu.roll(m, LANES - 1, 1) for m in middle[1:]]
    for c in range(columns):
        u = middle[c + 1]
        left = jnp.where(is_first, right_moved[c], right_moved[c + 1])
        right = jnp.where(is_last, left_moved[c + 1], left_moved[c])
        above = source[c, pl.ds(row - 1, ROWS), :]
        below = source[c, pl.ds(row + 1, ROWS), :]
        near = (above + below) + (left + right)
        result = u * (0.7 - DT * (u * u)) + (DT * near + force[c, pl.ds(force_row, ROWS), :])
        target[c, pl.ds(out_row, ROWS), :] = result
        if keep is not None:
            keep[c, pl.ds(keep_row, ROWS), :] = result


def halo_kernel(string, tilt, first, second, sems):
    odd = is_odd("slab")
    last = string.shape[1] - ROWS
    copies = []
    for n, (out, row) in enumerate(((first, (1 - odd) * last), (second, odd * last))):
        rows = pl.ds(pl.multiple_of(row, ROWS), ROWS)
        copies.append(pltpu.make_async_copy(string.at[:, rows], out.at[pl.ds(0, 2)], sems.at[2 * n]))
        copies.append(pltpu.make_async_copy(tilt.at[rows], out.at[2], sems.at[2 * n + 1]))
    for copy in copies:
        copy.start()
    for copy in copies:
        copy.wait()


def inner_kernel(string, tilt, full, history, edge_force, even, odd, force):
    depth = string.shape[1]
    columns = string.shape[2] // LANES
    bottom = 2 * SUBSTEPS - 2
    for c in range(columns):
        place = pl.ds(c * LANES, LANES)
        for image in range(2):
            rows = string[image, :, place]
            even[image, c] = rows
            history[0, image, c, pl.ds(0, ROWS), :] = rows[:ROWS]
            history[1, image, c, pl.ds(bottom, ROWS), :] = rows[depth - ROWS :]
        scaled = DT * tilt[:, place]
        force[c] = scaled
        edge_force[0, c] = scaled[:ROWS]
        edge_force[1, c] = scaled[depth - ROWS :]
    buffers = (even, odd)
    for step in range(1, SUBSTEPS + 1):
        source, target = buffers[(step - 1) % 2], buffers[step % 2]
        if step == SUBSTEPS:
            target = full
        last = depth - step - ROWS
        for image in range(2):
            for row in sorted(set(list(range(step, last, ROWS)) + [last])):
                keep, keep_row = None, 0
                if step < SUBSTEPS and row == step:
                    keep, keep_row = history.at[0, image], 2 * step
                if step < SUBSTEPS and row == last:
                    keep, keep_row = history.at[1, image], bottom - 2 * step
                substep(source.at[image], target.at[image], force, row, row, row, columns, keep, keep_row)


def edge_rows(side, halo, history, edge_force, full, even, odd, force):
    columns, depth = full.shape[1:3]
    mine, theirs = ((ROWS, 0), (0, ROWS))[side]
    for c in range(columns):
        place = pl.ds(c * LANES, LANES)
        for image in range(2):
            even[image, c, pl.ds(theirs, ROWS), :] = halo[image, :, place]
        force[c, pl.ds(theirs, ROWS), :] = DT * halo[2, :, place]
        force[c, pl.ds(mine, ROWS), :] = edge_force[side, c]
    buffers = (even, odd)
    for step in range(1, SUBSTEPS + 1):
        source, target = buffers[(step - 1) % 2], buffers[step % 2]
        out_row = theirs
        if step == SUBSTEPS:
            target, out_row = full, side * (depth - ROWS)
        kept = 2 * (step - 1) if side == 0 else 2 * SUBSTEPS + 4 - 2 * (step - 1)
        row, force_row = (1, step) if side == 0 else (ROWS - 1, ROWS - step)
        for image in range(2):
            for c in range(columns):
                source[image, c, pl.ds(ROWS - 2 * side, 2), :] = history[side, image, c, pl.ds(kept, 2), :]
            substep(source.at[image], target.at[image], force, row, out_row, force_row, columns)


def edge_kernel(is_second, halo, history, edge_force, inner, full, sent, even, odd, force):
    depth = full.shape[2]
    inside = depth - 2 * ROWS
    for side in range(2):

        @pl.when(is_odd("slab") == (side if is_second else 1 - side))
        def one():
            edge_rows(side, halo, history, edge_force, full, even, odd, force)
            rows = full[0, :, pl.ds(side * (depth - ROWS), ROWS), :]
            sent[:, pl.ds(0 if is_second else inside, ROWS), :] = rows

    if not is_second:
        sent[:, pl.ds(0, inside), :] = full[0, :, pl.ds(ROWS, inside), :]


def differences(upper, lower, columns, sums):
    def one(c, total):
        difference = upper(c) - lower(c)
        return total + difference * difference

    return lax.fori_loop(0, columns, one, sums, unroll=8)


def local_kernel(images, sources, full, early_high, sums, plan):
    columns, depth = full.shape[1:3]
    odd = odd_mask()
    upper, lower = pl.ds(0, ROWS), pl.ds(depth - ROWS, ROWS)
    inside = depth - 2 * ROWS
    zero = jnp.zeros((depth, LANES), jnp.float32)
    sums[0] = differences(lambda c: full[1, c], lambda c: full[0, c], columns, zero)
    sums[1] = zero
    sums[1, pl.ds(0, inside), :] = differences(
        lambda c: early_high[c, pl.ds(0, inside)], lambda c: full[1, c, pl.ds(ROWS, inside)], columns, zero[:inside]
    )
    sums[1, pl.ds(inside, ROWS), :] = differences(
        lambda c: early_high[c, pl.ds(inside, ROWS)],
        lambda c: jnp.where(odd, full[1, c, upper], full[1, c, lower]),
        columns,
        zero[:ROWS],
    )
    shape = plan.shape[2:]
    lane = lax.broadcasted_iota(jnp.int32, shape, 1)
    index = 2 * lax.broadcasted_iota(jnp.int32, shape, 0) + lane
    used = (lane < 2) & (index < images - 1)
    first = 2 * lax.axis_index("image")
    for t in range(2):
        target = first + t
        source = sources[target]
        place = source - (first - 2)
        plan[t, 0] = jnp.where(used & (index < source), 1.0, 0.0)
        plan[t, 1] = jnp.where(used & (index == source), 1.0, 0.0)
        plan[t, 2] = jnp.full(shape, target.astype(jnp.float32) / (images - 1))
        for m in range(5):
            plan[t, 3 + m] = jnp.full(shape, jnp.where(place == m, 1.0, 0.0))
            plan[t, 8 + m] = jnp.full(shape, jnp.where(place + 1 == m, 1.0, 0.0))


def square_kernel(sums, full, late_high, out):
    columns, depth = full.shape[1:3]
    odd = odd_mask()
    upper, lower = pl.ds(0, ROWS), pl.ds(depth - ROWS, ROWS)
    beyond = differences(
        lambda c: late_high[c],
        lambda c: jnp.where(odd, full[1, c, lower], full[1, c, upper]),
        columns,
        jnp.sum(sums[1].reshape(-1, ROWS, LANES), axis=0),
    )
    after = jnp.sum(sums[0], axis=(0, 1), keepdims=True)
    beyond = jnp.sum(beyond, axis=(0, 1), keepdims=True)
    lane = lax.broadcasted_iota(jnp.int32, (1, LANES), 1)
    row = jnp.where(lane == 0, after, jnp.where(lane == 1, beyond, 0.0))
    out[...] = jnp.broadcast_to(row[None], out.shape)


def total_kernel(parts, full_low, out):
    out[...] = jnp.broadcast_to(jnp.sum(parts[...], axis=0, keepdims=True), out.shape)


def mix_kernel(cells, images, squares, plan, full, full_low, early_high, late_high, out, mixed, sems):
    columns, depth = full.shape[1:3]
    rows = squares.shape[0]
    seg = jnp.sqrt(squares[...].reshape(rows, LANES) / cells + EPS)
    lane = lax.broadcasted_iota(jnp.int32, (rows, LANES), 1)
    index = 2 * lax.broadcasted_iota(jnp.int32, (rows, LANES), 0) + lane
    seg = jnp.where((lane < 2) & (index < images - 1), seg, 0.0)

    def whole(values):
        return jnp.sum(values, axis=(0, 1), keepdims=True)

    total = whole(seg)
    shares = []
    for t in range(2):
        weight = (plan[t, 2] * total - whole(plan[t, 0] * seg)) / whole(plan[t, 1] * seg)
        shares.append([(1.0 - weight) * plan[t, 3 + m] + weight * plan[t, 8 + m] for m in range(5)])
    odd = odd_mask()
    group = columns // 4
    copies = []
    for g in range(4):
        for c in range(g * group, (g + 1) * group):
            place = pl.ds(c * LANES, LANES)
            early, late = early_high[c, pl.ds(depth - 2 * ROWS, ROWS)], late_high[c]
            for high, row in (
                (jnp.where(odd, early, late), 0),
                (early_high[c, pl.ds(0, ROWS)], ROWS),
                (early_high[c, pl.ds(ROWS, ROWS)], 2 * ROWS),
                (jnp.where(odd, late, early), depth - ROWS),
            ):
                at = pl.ds(row, ROWS)
                fields = [full_low[0, c, at], full_low[1, c, at], full[0, c, at], full[1, c, at], high]
                for t in range(2):
                    result = shares[t][0] * fields[0]
                    for m in range(1, 5):
                        result = result + shares[t][m] * fields[m]
                    mixed[t, at, place] = result
        span = pl.ds(g * group * LANES, group * LANES)
        copy = pltpu.make_async_copy(mixed.at[:, :, span], out.at[:, :, span], sems.at[g])
        copy.start()
        copies.append(copy)
    for copy in copies:
        copy.wait()


VMEM = pl.BlockSpec(memory_space=pltpu.VMEM)
SMEM = pl.BlockSpec(memory_space=pltpu.SMEM)
HBM = pl.BlockSpec(memory_space=pltpu.HBM)
ANY = pl.BlockSpec(memory_space=pl.ANY)


def call(name, kernel, shapes, ins, scratch=(), outs=VMEM, cost=0, limit=VMEM_LIMIT, aliases=None):
    return pl.pallas_call(
        kernel,
        out_shape=shapes,
        in_specs=ins,
        out_specs=jax.tree.map(lambda _: outs, shapes),
        scratch_shapes=list(scratch),
        name=name,
        input_output_aliases=aliases or {},
        cost_estimate=pl.CostEstimate(flops=cost, bytes_accessed=1 << 20, transcendentals=0),
        compiler_params=pltpu.CompilerParams(vmem_limit_bytes=limit),
    )


def body(string, tilt, source_pair):
    count, depth, width = string.shape
    columns = width // LANES
    slabs = lax.axis_size("slab")
    ranks = lax.axis_size("image")
    images = count * ranks
    half = 2 * ROWS

    def array(*shape):
        return jax.ShapeDtypeStruct(shape, jnp.float32)

    def room(*shape):
        return pltpu.VMEM(shape, jnp.float32)

    halo = array(3, ROWS, width)
    first, second = call(
        "halo", halo_kernel, (halo, halo), [HBM] * 2, [pltpu.SemaphoreType.DMA((4,))], limit=HALO_LIMIT
    )(string, tilt)
    first = lax.ppermute(first, "slab", partners("slab", True))
    second = lax.ppermute(second, "slab", partners("slab", False))
    whole = array(2, columns, depth, LANES)
    full, history, edge_force = call(
        "inner",
        inner_kernel,
        (whole, array(2, 2, columns, 3 * ROWS, LANES), array(2, columns, ROWS, LANES)),
        [VMEM] * 2,
        [room(2, columns, depth, LANES), room(2, columns, depth, LANES), room(columns, depth, LANES)],
        cost=1 << 31,
    )(string, tilt)
    scratch = [room(2, columns, half, LANES), room(2, columns, half, LANES), room(columns, half, LANES)]

    def edge(name, is_second, received, full):
        rows = ROWS if is_second else depth - ROWS
        return call(
            name,
            functools.partial(edge_kernel, is_second),
            (whole, array(columns, rows, LANES)),
            [VMEM] * 4,
            scratch,
            cost=1 << 30 if is_second else 1 << 32,
            aliases={3: 0},
        )(received, history, edge_force, full)

    full, early = edge("edge_first", False, first, full)
    early_high = lax.ppermute(early, "image", line("image", -1))
    full, late = edge("edge_second", True, second, full)
    late_high = lax.ppermute(late, "image", line("image", -1))
    full_low = lax.ppermute(full, "image", line("image", 1))
    sums, plan = call(
        "local",
        functools.partial(local_kernel, images),
        (array(2, depth, LANES), array(2, 13, ranks, LANES)),
        [SMEM] + [VMEM] * 2,
        cost=1 << 28,
    )(source_pair, full, early_high)
    parts = call("square", square_kernel, array(slabs, 1, LANES), [VMEM] * 3, cost=3 << 32)(sums, full, late_high)
    parts = lax.all_to_all(parts, "slab", 0, 0)
    squares = call("total", total_kernel, array(ranks, 1, LANES), [VMEM, ANY], cost=1 << 33)(parts, full_low)
    squares = lax.all_to_all(squares, "image", 0, 0)
    cells = depth * slabs * width
    return call(
        "mix",
        functools.partial(mix_kernel, cells, images),
        array(*string.shape),
        [VMEM] * 6,
        [room(*string.shape), pltpu.SemaphoreType.DMA((4,))],
        outs=ANY,
    )(squares, plan, full, full_low, early_high, late_high)


def solution(mesh):
    placed = (P("image", "slab", None), P("slab", None), P())
    return jax.shard_map(
        body, mesh=mesh, in_specs=placed, out_specs=P("image", "slab", None), check_vma=False
    )
```

```python
import functools

import jax
import jax.numpy as jnp
from jax import lax
from jax.experimental import pallas as pl
from jax.experimental.pallas import tpu as pltpu
from jax.sharding import PartitionSpec as P

SUBSTEPS = 8
DT = 0.1
EPS = 1e-06
LANES = 128
ROWS = 8
VMEM_LIMIT = 48 * 1024 * 1024
HALO_LIMIT = 54136 * 1024


def partners(axis, first):
    count = lax.axis_size(axis)
    step = 1 if first else -1
    evens = range(0, count, 2)
    return [(i, (i + step) % count) for i in evens] + [((i + step) % count, i) for i in evens]


def line(axis, distance):
    devices = range(lax.axis_size(axis))
    return [(i, i + distance) for i in devices if i + distance in devices]


def is_odd(axis):
    return lax.rem(lax.axis_index(axis), 2)


def substep(source, target, force, row, out_row, force_row, columns, keep=None, keep_row=0):
    lane = lax.broadcasted_iota(jnp.int32, (ROWS, LANES), 1)
    is_first = lane == 0
    is_last = lane == LANES - 1
    middle = [source[c % columns, pl.ds(row, ROWS), :] for c in range(-1, columns + 1)]
    right_moved = [pltpu.roll(m, 1, 1) for m in middle[:-1]]
    left_moved = [pltpu.roll(m, LANES - 1, 1) for m in middle[1:]]
    for c in range(columns):
        u = middle[c + 1]
        left = jnp.where(is_first, right_moved[c], right_moved[c + 1])
        right = jnp.where(is_last, left_moved[c + 1], left_moved[c])
        above = source[c, pl.ds(row - 1, ROWS), :]
        below = source[c, pl.ds(row + 1, ROWS), :]
        near = (above + below) + (left + right)
        result = u * (0.7 - DT * (u * u)) + (DT * near + force[c, pl.ds(force_row, ROWS), :])
        target[c, pl.ds(out_row, ROWS), :] = result
        if keep is not None:
            keep[c, pl.ds(keep_row, ROWS), :] = result


def halo_kernel(string, tilt, first, second, sems):
    odd = is_odd("slab")
    last = string.shape[1] - ROWS
    copies = []
    for n, (out, row) in enumerate(((first, (1 - odd) * last), (second, odd * last))):
        rows = pl.ds(pl.multiple_of(row, ROWS), ROWS)
        copies.append(pltpu.make_async_copy(string.at[:, rows], out.at[pl.ds(0, 2)], sems.at[2 * n]))
        copies.append(pltpu.make_async_copy(tilt.at[rows], out.at[2], sems.at[2 * n + 1]))
    for copy in copies:
        copy.start()
    for copy in copies:
        copy.wait()


def inner_kernel(string, tilt, full, middle, history, edge_force, even, odd, force):
    depth = string.shape[1]
    columns = string.shape[2] // LANES
    bottom = 2 * SUBSTEPS - 2
    for c in range(columns):
        place = pl.ds(c * LANES, LANES)
        for image in range(2):
            rows = string[image, :, place]
            even[image, c] = rows
            history[0, image, c, pl.ds(0, ROWS), :] = rows[:ROWS]
            history[1, image, c, pl.ds(bottom, ROWS), :] = rows[depth - ROWS :]
        scaled = DT * tilt[:, place]
        force[c] = scaled
        edge_force[0, c] = scaled[:ROWS]
        edge_force[1, c] = scaled[depth - ROWS :]
    buffers = (even, odd)
    for step in range(1, SUBSTEPS + 1):
        source, target = buffers[(step - 1) % 2], buffers[step % 2]
        if step == SUBSTEPS:
            target = full
        last = depth - step - ROWS
        for image in range(2):
            for row in sorted(set(list(range(step, last, ROWS)) + [last])):
                keep, keep_row = None, 0
                if step < SUBSTEPS and row == step:
                    keep, keep_row = history.at[0, image], 2 * step
                if step < SUBSTEPS and row == last:
                    keep, keep_row = history.at[1, image], bottom - 2 * step
                substep(source.at[image], target.at[image], force, row, row, row, columns, keep, keep_row)
    middle[...] = full[0, :, pl.ds(ROWS, depth - 2 * ROWS), :]


def edge_rows(side, halo, history, edge_force, full, even, odd, force):
    columns, depth = full.shape[1:3]
    mine, theirs = ((ROWS, 0), (0, ROWS))[side]
    for c in range(columns):
        place = pl.ds(c * LANES, LANES)
        for image in range(2):
            even[image, c, pl.ds(theirs, ROWS), :] = halo[image, :, place]
        force[c, pl.ds(theirs, ROWS), :] = DT * halo[2, :, place]
        force[c, pl.ds(mine, ROWS), :] = edge_force[side, c]
    buffers = (even, odd)
    for step in range(1, SUBSTEPS + 1):
        source, target = buffers[(step - 1) % 2], buffers[step % 2]
        out_row = theirs
        if step == SUBSTEPS:
            target, out_row = full, side * (depth - ROWS)
        kept = 2 * (step - 1) if side == 0 else 2 * SUBSTEPS + 4 - 2 * (step - 1)
        row, force_row = (1, step) if side == 0 else (ROWS - 1, ROWS - step)
        for image in range(2):
            for c in range(columns):
                source[image, c, pl.ds(ROWS - 2 * side, 2), :] = history[side, image, c, pl.ds(kept, 2), :]
            substep(source.at[image], target.at[image], force, row, out_row, force_row, columns)


def edge_kernel(is_second, halo, history, edge_force, inner, full, *rest):
    even, odd, force = rest[-3:]
    depth = full.shape[2]
    for side in range(2):

        @pl.when(is_odd("slab") == (side if is_second else 1 - side))
        def one():
            edge_rows(side, halo, history, edge_force, full, even, odd, force)

    if is_second:
        edges = rest[0]
        edges[:, pl.ds(0, ROWS), :] = full[0, :, pl.ds(0, ROWS), :]
        edges[:, pl.ds(ROWS, ROWS), :] = full[0, :, pl.ds(depth - ROWS, ROWS), :]


def differences(upper, lower, columns, sums):
    def one(c, total):
        difference = upper(c) - lower(c)
        return total + difference * difference

    return lax.fori_loop(0, columns, one, sums, unroll=8)


def local_kernel(images, sources, full, middle_high, sums, plan):
    columns, depth = full.shape[1:3]
    inside = depth - 2 * ROWS
    zero = jnp.zeros((depth, LANES), jnp.float32)
    sums[pl.ds(0, depth), :] = differences(lambda c: full[1, c], lambda c: full[0, c], columns, zero)
    sums[pl.ds(depth, inside), :] = differences(
        lambda c: middle_high[c], lambda c: full[1, c, pl.ds(ROWS, inside)], columns, zero[:inside]
    )
    shape = plan.shape[2:]
    lane = lax.broadcasted_iota(jnp.int32, shape, 1)
    index = 2 * lax.broadcasted_iota(jnp.int32, shape, 0) + lane
    used = (lane < 2) & (index < images - 1)
    first = 2 * lax.axis_index("image")
    for t in range(2):
        target = first + t
        source = sources[target]
        place = source - (first - 2)
        plan[t, 0] = jnp.where(used & (index < source), 1.0, 0.0)
        plan[t, 1] = jnp.where(used & (index == source), 1.0, 0.0)
        plan[t, 2] = jnp.full(shape, target.astype(jnp.float32) / (images - 1))
        for m in range(5):
            plan[t, 3 + m] = jnp.full(shape, jnp.where(place == m, 1.0, 0.0))
            plan[t, 8 + m] = jnp.full(shape, jnp.where(place + 1 == m, 1.0, 0.0))


def square_kernel(sums, full, edges_high, out):
    columns, depth = full.shape[1:3]
    beyond = sums[pl.ds(depth, ROWS), :] + sums[pl.ds(depth + ROWS, ROWS), :]
    for row, at in ((0, 0), (ROWS, depth - ROWS)):
        beyond = differences(
            lambda c: edges_high[c, pl.ds(row, ROWS)], lambda c: full[1, c, pl.ds(at, ROWS)], columns, beyond
        )
    after = jnp.sum(sums[pl.ds(0, depth), :], axis=(0, 1), keepdims=True)
    beyond = jnp.sum(beyond, axis=(0, 1), keepdims=True)
    lane = lax.broadcasted_iota(jnp.int32, (1, LANES), 1)
    row = jnp.where(lane == 0, after, jnp.where(lane == 1, beyond, 0.0))
    out[...] = jnp.broadcast_to(row[None], out.shape)


def total_kernel(parts, full_low, out):
    out[...] = jnp.broadcast_to(jnp.sum(parts[...], axis=0, keepdims=True), out.shape)


def mix_kernel(cells, images, squares, plan, full, full_low, middle_high, edges_high, out, mixed, sems):
    columns, depth = full.shape[1:3]
    rows = squares.shape[0]
    seg = jnp.sqrt(squares[...].reshape(rows, LANES) / cells + EPS)
    lane = lax.broadcasted_iota(jnp.int32, (rows, LANES), 1)
    index = 2 * lax.broadcasted_iota(jnp.int32, (rows, LANES), 0) + lane
    seg = jnp.where((lane < 2) & (index < images - 1), seg, 0.0)

    def whole(values):
        return jnp.sum(values, axis=(0, 1), keepdims=True)

    total = whole(seg)
    shares = []
    for t in range(2):
        weight = (plan[t, 2] * total - whole(plan[t, 0] * seg)) / whole(plan[t, 1] * seg)
        shares.append([(1.0 - weight) * plan[t, 3 + m] + weight * plan[t, 8 + m] for m in range(5)])
    group = columns // 4
    copies = []
    for g in range(4):
        for c in range(g * group, (g + 1) * group):
            place = pl.ds(c * LANES, LANES)
            for high, row, at in (
                (edges_high, 0, 0),
                (middle_high, 0, ROWS),
                (middle_high, ROWS, 2 * ROWS),
                (edges_high, ROWS, depth - ROWS),
            ):
                high = high[c, pl.ds(row, ROWS)]
                at = pl.ds(at, ROWS)
                fields = [full_low[0, c, at], full_low[1, c, at], full[0, c, at], full[1, c, at], high]
                for t in range(2):
                    result = shares[t][0] * fields[0]
                    for m in range(1, 5):
                        result = result + shares[t][m] * fields[m]
                    mixed[t, at, place] = result
        span = pl.ds(g * group * LANES, group * LANES)
        copy = pltpu.make_async_copy(mixed.at[:, :, span], out.at[:, :, span], sems.at[g])
        copy.start()
        copies.append(copy)
    for copy in copies:
        copy.wait()


VMEM = pl.BlockSpec(memory_space=pltpu.VMEM)
SMEM = pl.BlockSpec(memory_space=pltpu.SMEM)
HBM = pl.BlockSpec(memory_space=pltpu.HBM)
ANY = pl.BlockSpec(memory_space=pl.ANY)


def call(name, kernel, shapes, ins, scratch=(), outs=VMEM, cost=0, limit=VMEM_LIMIT, aliases=None):
    return pl.pallas_call(
        kernel,
        out_shape=shapes,
        in_specs=ins,
        out_specs=jax.tree.map(lambda _: outs, shapes),
        scratch_shapes=list(scratch),
        name=name,
        input_output_aliases=aliases or {},
        cost_estimate=pl.CostEstimate(flops=cost, bytes_accessed=1 << 20, transcendentals=0),
        compiler_params=pltpu.CompilerParams(vmem_limit_bytes=limit),
    )


def body(string, tilt, source_pair):
    count, depth, width = string.shape
    columns = width // LANES
    slabs = lax.axis_size("slab")
    ranks = lax.axis_size("image")
    images = count * ranks
    half = 2 * ROWS

    def array(*shape):
        return jax.ShapeDtypeStruct(shape, jnp.float32)

    def room(*shape):
        return pltpu.VMEM(shape, jnp.float32)

    halo = array(3, ROWS, width)
    first, second = call(
        "halo", halo_kernel, (halo, halo), [HBM] * 2, [pltpu.SemaphoreType.DMA((4,))], limit=HALO_LIMIT
    )(string, tilt)
    first = lax.ppermute(first, "slab", partners("slab", True))
    second = lax.ppermute(second, "slab", partners("slab", False))
    whole = array(2, columns, depth, LANES)
    single = array(columns, half, LANES)
    full, middle, history, edge_force = call(
        "inner",
        inner_kernel,
        (whole, single, array(2, 2, columns, 3 * ROWS, LANES), array(2, columns, ROWS, LANES)),
        [VMEM] * 2,
        [room(2, columns, depth, LANES), room(2, columns, depth, LANES), room(columns, depth, LANES)],
        cost=1 << 31,
    )(string, tilt)
    middle_high = lax.ppermute(middle, "image", line("image", -1))

    def edge(name, is_second, received, full):
        return call(
            name,
            functools.partial(edge_kernel, is_second),
            (whole, single) if is_second else (whole,),
            [VMEM] * 4,
            [room(2, columns, half, LANES), room(2, columns, half, LANES), room(columns, half, LANES)],
            cost=1 << 30 if is_second else 1 << 32,
            aliases={3: 0},
        )(received, history, edge_force, full)

    (full,) = edge("edge_first", False, first, full)
    full, edges = edge("edge_second", True, second, full)
    edges_high = lax.ppermute(edges, "image", line("image", -1))
    full_low = lax.ppermute(full, "image", line("image", 1))
    sums, plan = call(
        "local",
        functools.partial(local_kernel, images),
        (array(depth + half, LANES), array(2, 13, ranks, LANES)),
        [SMEM] + [VMEM] * 2,
        cost=1 << 28,
    )(source_pair, full, middle_high)
    parts = call("square", square_kernel, array(slabs, 1, LANES), [VMEM] * 3, cost=3 << 32)(sums, full, edges_high)
    parts = lax.all_to_all(parts, "slab", 0, 0)
    squares = call("total", total_kernel, array(ranks, 1, LANES), [VMEM, ANY], cost=1 << 33)(parts, full_low)
    squares = lax.all_to_all(squares, "image", 0, 0)
    cells = depth * slabs * width
    return call(
        "mix",
        functools.partial(mix_kernel, cells, images),
        array(*string.shape),
        [VMEM] * 6,
        [room(*string.shape), pltpu.SemaphoreType.DMA((4,))],
        outs=ANY,
    )(squares, plan, full, full_low, middle_high, edges_high)


def solution(mesh):
    placed = (P("image", "slab", None), P("slab", None), P())
    return jax.shard_map(
        body, mesh=mesh, in_specs=placed, out_specs=P("image", "slab", None), check_vma=False
    )
```

```python
import functools

import jax
import jax.numpy as jnp
from jax import lax
from jax.experimental import pallas as pl
from jax.experimental.pallas import tpu as pltpu
from jax.sharding import PartitionSpec as P

SUBSTEPS = 8
DT = 0.1
EPS = 1e-06
LANES = 128
ROWS = 8
VMEM_LIMIT = 48 * 1024 * 1024
HALO_LIMIT = 54136 * 1024


def partners(axis, first):
    count = lax.axis_size(axis)
    step = -1 if first else 1
    evens = range(0, count, 2)
    return [(i, (i + step) % count) for i in evens] + [((i + step) % count, i) for i in evens]


def line(axis, distance):
    devices = range(lax.axis_size(axis))
    return [(i, i + distance) for i in devices if i + distance in devices]


def is_odd(axis):
    return lax.rem(lax.axis_index(axis), 2)


def substep(source, target, force, row, out_row, force_row, columns, keep=None, keep_row=0):
    lane = lax.broadcasted_iota(jnp.int32, (ROWS, LANES), 1)
    is_first = lane == 0
    is_last = lane == LANES - 1
    middle = [source[c % columns, pl.ds(row, ROWS), :] for c in range(-1, columns + 1)]
    right_moved = [pltpu.roll(m, 1, 1) for m in middle[:-1]]
    left_moved = [pltpu.roll(m, LANES - 1, 1) for m in middle[1:]]
    for c in range(columns):
        u = middle[c + 1]
        left = jnp.where(is_first, right_moved[c], right_moved[c + 1])
        right = jnp.where(is_last, left_moved[c + 1], left_moved[c])
        above = source[c, pl.ds(row - 1, ROWS), :]
        below = source[c, pl.ds(row + 1, ROWS), :]
        near = (above + below) + (left + right)
        result = u * (0.7 - DT * (u * u)) + (DT * near + force[c, pl.ds(force_row, ROWS), :])
        target[c, pl.ds(out_row, ROWS), :] = result
        if keep is not None:
            keep[c, pl.ds(keep_row, ROWS), :] = result


def halo_kernel(string, tilt, first, second, sems):
    odd = is_odd("slab")
    last = string.shape[1] - ROWS
    copies = []
    for n, (out, row) in enumerate(((first, odd * last), (second, (1 - odd) * last))):
        rows = pl.ds(pl.multiple_of(row, ROWS), ROWS)
        copies.append(pltpu.make_async_copy(string.at[:, rows], out.at[pl.ds(0, 2)], sems.at[2 * n]))
        copies.append(pltpu.make_async_copy(tilt.at[rows], out.at[2], sems.at[2 * n + 1]))
    for copy in copies:
        copy.start()
    for copy in copies:
        copy.wait()


def inner_kernel(string, tilt, full, middle, history, edge_force, even, odd, force):
    depth = string.shape[1]
    columns = string.shape[2] // LANES
    bottom = 2 * SUBSTEPS - 2
    for c in range(columns):
        place = pl.ds(c * LANES, LANES)
        for image in range(2):
            rows = string[image, :, place]
            even[image, c] = rows
            history[0, image, c, pl.ds(0, ROWS), :] = rows[:ROWS]
            history[1, image, c, pl.ds(bottom, ROWS), :] = rows[depth - ROWS :]
        scaled = DT * tilt[:, place]
        force[c] = scaled
        edge_force[0, c] = scaled[:ROWS]
        edge_force[1, c] = scaled[depth - ROWS :]
    buffers = (even, odd)
    for step in range(1, SUBSTEPS + 1):
        source, target = buffers[(step - 1) % 2], buffers[step % 2]
        if step == SUBSTEPS:
            target = full
        last = depth - step - ROWS
        for image in range(2):
            for row in sorted(set(list(range(step, last, ROWS)) + [last])):
                keep, keep_row = None, 0
                if step < SUBSTEPS and row == step:
                    keep, keep_row = history.at[0, image], 2 * step
                if step < SUBSTEPS and row == last:
                    keep, keep_row = history.at[1, image], bottom - 2 * step
                substep(source.at[image], target.at[image], force, row, row, row, columns, keep, keep_row)
    middle[...] = full[0, :, pl.ds(ROWS, depth - 2 * ROWS), :]


def edge_rows(side, halo, history, edge_force, full, even, odd, force):
    columns, depth = full.shape[1:3]
    mine, theirs = ((ROWS, 0), (0, ROWS))[side]
    for c in range(columns):
        place = pl.ds(c * LANES, LANES)
        for image in range(2):
            even[image, c, pl.ds(theirs, ROWS), :] = halo[image, :, place]
        force[c, pl.ds(theirs, ROWS), :] = DT * halo[2, :, place]
        force[c, pl.ds(mine, ROWS), :] = edge_force[side, c]
    buffers = (even, odd)
    for step in range(1, SUBSTEPS + 1):
        source, target = buffers[(step - 1) % 2], buffers[step % 2]
        out_row = theirs
        if step == SUBSTEPS:
            target, out_row = full, side * (depth - ROWS)
        kept = 2 * (step - 1) if side == 0 else 2 * SUBSTEPS + 4 - 2 * (step - 1)
        row, force_row = (1, step) if side == 0 else (ROWS - 1, ROWS - step)
        for image in range(2):
            for c in range(columns):
                source[image, c, pl.ds(ROWS - 2 * side, 2), :] = history[side, image, c, pl.ds(kept, 2), :]
            substep(source.at[image], target.at[image], force, row, out_row, force_row, columns)


def edge_kernel(is_second, halo, history, edge_force, inner, full, *rest):
    even, odd, force = rest[-3:]
    depth = full.shape[2]
    for side in range(2):

        @pl.when(is_odd("slab") == (1 - side if is_second else side))
        def one():
            edge_rows(side, halo, history, edge_force, full, even, odd, force)

    if is_second:
        edges = rest[0]
        edges[:, pl.ds(0, ROWS), :] = full[0, :, pl.ds(0, ROWS), :]
        edges[:, pl.ds(ROWS, ROWS), :] = full[0, :, pl.ds(depth - ROWS, ROWS), :]


def differences(upper, lower, columns, sums):
    def one(c, total):
        difference = upper(c) - lower(c)
        return total + difference * difference

    return lax.fori_loop(0, columns, one, sums, unroll=8)


def local_kernel(images, sources, full, middle_high, sums, plan):
    columns, depth = full.shape[1:3]
    inside = depth - 2 * ROWS
    zero = jnp.zeros((depth, LANES), jnp.float32)
    sums[pl.ds(0, depth), :] = differences(lambda c: full[1, c], lambda c: full[0, c], columns, zero)
    sums[pl.ds(depth, inside), :] = differences(
        lambda c: middle_high[c], lambda c: full[1, c, pl.ds(ROWS, inside)], columns, zero[:inside]
    )
    shape = plan.shape[2:]
    lane = lax.broadcasted_iota(jnp.int32, shape, 1)
    index = 2 * lax.broadcasted_iota(jnp.int32, shape, 0) + lane
    used = (lane < 2) & (index < images - 1)
    first = 2 * lax.axis_index("image")
    for t in range(2):
        target = first + t
        source = sources[target]
        place = source - (first - 2)
        plan[t, 0] = jnp.where(used & (index < source), 1.0, 0.0)
        plan[t, 1] = jnp.where(used & (index == source), 1.0, 0.0)
        plan[t, 2] = jnp.full(shape, target.astype(jnp.float32) / (images - 1))
        for m in range(5):
            plan[t, 3 + m] = jnp.full(shape, jnp.where(place == m, 1.0, 0.0))
            plan[t, 8 + m] = jnp.full(shape, jnp.where(place + 1 == m, 1.0, 0.0))


def square_kernel(sums, full, edges_high, out):
    columns, depth = full.shape[1:3]
    beyond = sums[pl.ds(depth, ROWS), :] + sums[pl.ds(depth + ROWS, ROWS), :]
    for row, at in ((0, 0), (ROWS, depth - ROWS)):
        beyond = differences(
            lambda c: edges_high[c, pl.ds(row, ROWS)], lambda c: full[1, c, pl.ds(at, ROWS)], columns, beyond
        )
    after = jnp.sum(sums[pl.ds(0, depth), :], axis=(0, 1), keepdims=True)
    beyond = jnp.sum(beyond, axis=(0, 1), keepdims=True)
    lane = lax.broadcasted_iota(jnp.int32, (1, LANES), 1)
    row = jnp.where(lane == 0, after, jnp.where(lane == 1, beyond, 0.0))
    out[...] = jnp.broadcast_to(row[None], out.shape)


def total_kernel(parts, full_low, out):
    out[...] = jnp.broadcast_to(jnp.sum(parts[...], axis=0, keepdims=True), out.shape)


def mix_kernel(cells, images, squares, plan, full, full_low, middle_high, edges_high, out, mixed, sems):
    columns, depth = full.shape[1:3]
    rows = squares.shape[0]
    seg = jnp.sqrt(squares[...].reshape(rows, LANES) / cells + EPS)
    lane = lax.broadcasted_iota(jnp.int32, (rows, LANES), 1)
    index = 2 * lax.broadcasted_iota(jnp.int32, (rows, LANES), 0) + lane
    seg = jnp.where((lane < 2) & (index < images - 1), seg, 0.0)

    def whole(values):
        return jnp.sum(values, axis=(0, 1), keepdims=True)

    total = whole(seg)
    shares = []
    for t in range(2):
        weight = (plan[t, 2] * total - whole(plan[t, 0] * seg)) / whole(plan[t, 1] * seg)
        shares.append([(1.0 - weight) * plan[t, 3 + m] + weight * plan[t, 8 + m] for m in range(5)])
    group = columns // 4
    copies = []
    for g in range(4):
        for c in range(g * group, (g + 1) * group):
            place = pl.ds(c * LANES, LANES)
            for high, row, at in (
                (edges_high, 0, 0),
                (middle_high, 0, ROWS),
                (middle_high, ROWS, 2 * ROWS),
                (edges_high, ROWS, depth - ROWS),
            ):
                high = high[c, pl.ds(row, ROWS)]
                at = pl.ds(at, ROWS)
                fields = [full_low[0, c, at], full_low[1, c, at], full[0, c, at], full[1, c, at], high]
                for t in range(2):
                    result = shares[t][0] * fields[0]
                    for m in range(1, 5):
                        result = result + shares[t][m] * fields[m]
                    mixed[t, at, place] = result
        span = pl.ds(g * group * LANES, group * LANES)
        copy = pltpu.make_async_copy(mixed.at[:, :, span], out.at[:, :, span], sems.at[g])
        copy.start()
        copies.append(copy)
    for copy in copies:
        copy.wait()


VMEM = pl.BlockSpec(memory_space=pltpu.VMEM)
SMEM = pl.BlockSpec(memory_space=pltpu.SMEM)
HBM = pl.BlockSpec(memory_space=pltpu.HBM)
ANY = pl.BlockSpec(memory_space=pl.ANY)


def call(name, kernel, shapes, ins, scratch=(), outs=VMEM, cost=0, limit=VMEM_LIMIT, aliases=None):
    return pl.pallas_call(
        kernel,
        out_shape=shapes,
        in_specs=ins,
        out_specs=jax.tree.map(lambda _: outs, shapes),
        scratch_shapes=list(scratch),
        name=name,
        input_output_aliases=aliases or {},
        cost_estimate=pl.CostEstimate(flops=cost, bytes_accessed=1 << 20, transcendentals=0),
        compiler_params=pltpu.CompilerParams(vmem_limit_bytes=limit),
    )


def body(string, tilt, source_pair):
    count, depth, width = string.shape
    columns = width // LANES
    slabs = lax.axis_size("slab")
    ranks = lax.axis_size("image")
    images = count * ranks
    half = 2 * ROWS

    def array(*shape):
        return jax.ShapeDtypeStruct(shape, jnp.float32)

    def room(*shape):
        return pltpu.VMEM(shape, jnp.float32)

    halo = array(3, ROWS, width)
    first, second = call(
        "halo", halo_kernel, (halo, halo), [HBM] * 2, [pltpu.SemaphoreType.DMA((4,))], limit=HALO_LIMIT
    )(string, tilt)
    first = lax.ppermute(first, "slab", partners("slab", True))
    second = lax.ppermute(second, "slab", partners("slab", False))
    whole = array(2, columns, depth, LANES)
    single = array(columns, half, LANES)
    full, middle, history, edge_force = call(
        "inner",
        inner_kernel,
        (whole, single, array(2, 2, columns, 3 * ROWS, LANES), array(2, columns, ROWS, LANES)),
        [VMEM] * 2,
        [room(2, columns, depth, LANES), room(2, columns, depth, LANES), room(columns, depth, LANES)],
        cost=1 << 31,
    )(string, tilt)
    middle_high = lax.ppermute(middle, "image", line("image", -1))

    def edge(name, is_second, received, full):
        return call(
            name,
            functools.partial(edge_kernel, is_second),
            (whole, single) if is_second else (whole,),
            [VMEM] * 4,
            [room(2, columns, half, LANES), room(2, columns, half, LANES), room(columns, half, LANES)],
            cost=1 << 30 if is_second else 1 << 32,
            aliases={3: 0},
        )(received, history, edge_force, full)

    (full,) = edge("edge_first", False, first, full)
    full, edges = edge("edge_second", True, second, full)
    edges_high = lax.ppermute(edges, "image", line("image", -1))
    full_low = lax.ppermute(full, "image", line("image", 1))
    sums, plan = call(
        "local",
        functools.partial(local_kernel, images),
        (array(depth + half, LANES), array(2, 13, ranks, LANES)),
        [SMEM] + [VMEM] * 2,
        cost=1 << 28,
    )(source_pair, full, middle_high)
    parts = call("square", square_kernel, array(slabs, 1, LANES), [VMEM] * 3, cost=3 << 32)(sums, full, edges_high)
    parts = lax.all_to_all(parts, "slab", 0, 0)
    squares = call("total", total_kernel, array(ranks, 1, LANES), [VMEM, ANY], cost=1 << 33)(parts, full_low)
    squares = lax.all_to_all(squares, "image", 0, 0)
    cells = depth * slabs * width
    return call(
        "mix",
        functools.partial(mix_kernel, cells, images),
        array(*string.shape),
        [VMEM] * 6,
        [room(*string.shape), pltpu.SemaphoreType.DMA((4,))],
        outs=ANY,
    )(squares, plan, full, full_low, middle_high, edges_high)


def solution(mesh):
    placed = (P("image", "slab", None), P("slab", None), P())
    return jax.shard_map(
        body, mesh=mesh, in_specs=placed, out_specs=P("image", "slab", None), check_vma=False
    )
```

```python
import functools

import jax
import jax.numpy as jnp
from jax import lax
from jax.experimental import pallas as pl
from jax.experimental.pallas import tpu as pltpu
from jax.sharding import PartitionSpec as P

SUBSTEPS = 8
DT = 0.1
EPS = 1e-06
LANES = 128
ROWS = 8
VMEM_LIMIT = 48 * 1024 * 1024
HALO_LIMIT = 54136 * 1024


def partners(first):
    ranks, slabs = lax.axis_size("image"), lax.axis_size("slab")
    step = -1 if first else 1
    pairs = []
    for i in range(ranks):
        for s in range(i % 2, slabs, 2):
            here, there = i * slabs + s, i * slabs + (s + step) % slabs
            pairs += [(here, there), (there, here)]
    return pairs


def line(axis, distance):
    devices = range(lax.axis_size(axis))
    return [(i, i + distance) for i in devices if i + distance in devices]


def is_odd():
    return lax.rem(lax.axis_index("image") + lax.axis_index("slab"), 2)


def substep(source, target, force, row, out_row, force_row, columns, keep=None, keep_row=0):
    lane = lax.broadcasted_iota(jnp.int32, (ROWS, LANES), 1)
    is_first = lane == 0
    is_last = lane == LANES - 1
    middle = [source[c % columns, pl.ds(row, ROWS), :] for c in range(-1, columns + 1)]
    right_moved = [pltpu.roll(m, 1, 1) for m in middle[:-1]]
    left_moved = [pltpu.roll(m, LANES - 1, 1) for m in middle[1:]]
    for c in range(columns):
        u = middle[c + 1]
        left = jnp.where(is_first, right_moved[c], right_moved[c + 1])
        right = jnp.where(is_last, left_moved[c + 1], left_moved[c])
        above = source[c, pl.ds(row - 1, ROWS), :]
        below = source[c, pl.ds(row + 1, ROWS), :]
        near = (above + below) + (left + right)
        result = u * (0.7 - DT * (u * u)) + (DT * near + force[c, pl.ds(force_row, ROWS), :])
        target[c, pl.ds(out_row, ROWS), :] = result
        if keep is not None:
            keep[c, pl.ds(keep_row, ROWS), :] = result


def halo_kernel(string, tilt, first, second, sems):
    odd = is_odd()
    last = string.shape[1] - ROWS
    copies = []
    for n, (out, row) in enumerate(((first, odd * last), (second, (1 - odd) * last))):
        rows = pl.ds(pl.multiple_of(row, ROWS), ROWS)
        copies.append(pltpu.make_async_copy(string.at[:, rows], out.at[pl.ds(0, 2)], sems.at[2 * n]))
        copies.append(pltpu.make_async_copy(tilt.at[rows], out.at[2], sems.at[2 * n + 1]))
    for copy in copies:
        copy.start()
    for copy in copies:
        copy.wait()


def inner_kernel(string, tilt, full, middle, history, edge_force, even, odd, force):
    depth = string.shape[1]
    columns = string.shape[2] // LANES
    bottom = 2 * SUBSTEPS - 2
    for c in range(columns):
        place = pl.ds(c * LANES, LANES)
        for image in range(2):
            rows = string[image, :, place]
            even[image, c] = rows
            history[0, image, c, pl.ds(0, ROWS), :] = rows[:ROWS]
            history[1, image, c, pl.ds(bottom, ROWS), :] = rows[depth - ROWS :]
        scaled = DT * tilt[:, place]
        force[c] = scaled
        edge_force[0, c] = scaled[:ROWS]
        edge_force[1, c] = scaled[depth - ROWS :]
    buffers = (even, odd)
    for step in range(1, SUBSTEPS + 1):
        source, target = buffers[(step - 1) % 2], buffers[step % 2]
        if step == SUBSTEPS:
            target = full
        last = depth - step - ROWS
        for image in range(2):
            for row in sorted(set(list(range(step, last, ROWS)) + [last])):
                keep, keep_row = None, 0
                if step < SUBSTEPS and row == step:
                    keep, keep_row = history.at[0, image], 2 * step
                if step < SUBSTEPS and row == last:
                    keep, keep_row = history.at[1, image], bottom - 2 * step
                substep(source.at[image], target.at[image], force, row, row, row, columns, keep, keep_row)
    middle[...] = full[0, :, pl.ds(ROWS, depth - 2 * ROWS), :]


def edge_rows(side, halo, history, edge_force, full, even, odd, force):
    columns, depth = full.shape[1:3]
    mine, theirs = ((ROWS, 0), (0, ROWS))[side]
    for c in range(columns):
        place = pl.ds(c * LANES, LANES)
        for image in range(2):
            even[image, c, pl.ds(theirs, ROWS), :] = halo[image, :, place]
        force[c, pl.ds(theirs, ROWS), :] = DT * halo[2, :, place]
        force[c, pl.ds(mine, ROWS), :] = edge_force[side, c]
    buffers = (even, odd)
    for step in range(1, SUBSTEPS + 1):
        source, target = buffers[(step - 1) % 2], buffers[step % 2]
        out_row = theirs
        if step == SUBSTEPS:
            target, out_row = full, side * (depth - ROWS)
        kept = 2 * (step - 1) if side == 0 else 2 * SUBSTEPS + 4 - 2 * (step - 1)
        row, force_row = (1, step) if side == 0 else (ROWS - 1, ROWS - step)
        for image in range(2):
            for c in range(columns):
                source[image, c, pl.ds(ROWS - 2 * side, 2), :] = history[side, image, c, pl.ds(kept, 2), :]
            substep(source.at[image], target.at[image], force, row, out_row, force_row, columns)


def edge_kernel(is_second, halo, history, edge_force, inner, full, *rest):
    even, odd, force = rest[-3:]
    depth = full.shape[2]
    for side in range(2):

        @pl.when(is_odd() == (1 - side if is_second else side))
        def one():
            edge_rows(side, halo, history, edge_force, full, even, odd, force)

    if is_second:
        edges = rest[0]
        edges[:, pl.ds(0, ROWS), :] = full[0, :, pl.ds(0, ROWS), :]
        edges[:, pl.ds(ROWS, ROWS), :] = full[0, :, pl.ds(depth - ROWS, ROWS), :]


def differences(upper, lower, columns, sums):
    def one(c, total):
        difference = upper(c) - lower(c)
        return total + difference * difference

    return lax.fori_loop(0, columns, one, sums, unroll=8)


def local_kernel(images, sources, full, middle_high, sums, plan):
    columns, depth = full.shape[1:3]
    inside = depth - 2 * ROWS
    zero = jnp.zeros((depth, LANES), jnp.float32)
    sums[pl.ds(0, depth), :] = differences(lambda c: full[1, c], lambda c: full[0, c], columns, zero)
    sums[pl.ds(depth, inside), :] = differences(
        lambda c: middle_high[c], lambda c: full[1, c, pl.ds(ROWS, inside)], columns, zero[:inside]
    )
    shape = plan.shape[2:]
    lane = lax.broadcasted_iota(jnp.int32, shape, 1)
    index = 2 * lax.broadcasted_iota(jnp.int32, shape, 0) + lane
    used = (lane < 2) & (index < images - 1)
    first = 2 * lax.axis_index("image")
    for t in range(2):
        target = first + t
        source = sources[target]
        place = source - (first - 2)
        plan[t, 0] = jnp.where(used & (index < source), 1.0, 0.0)
        plan[t, 1] = jnp.where(used & (index == source), 1.0, 0.0)
        plan[t, 2] = jnp.full(shape, target.astype(jnp.float32) / (images - 1))
        for m in range(5):
            plan[t, 3 + m] = jnp.full(shape, jnp.where(place == m, 1.0, 0.0))
            plan[t, 8 + m] = jnp.full(shape, jnp.where(place + 1 == m, 1.0, 0.0))


def square_kernel(sums, full, edges_high, out):
    columns, depth = full.shape[1:3]
    beyond = sums[pl.ds(depth, ROWS), :] + sums[pl.ds(depth + ROWS, ROWS), :]
    for row, at in ((0, 0), (ROWS, depth - ROWS)):
        beyond = differences(
            lambda c: edges_high[c, pl.ds(row, ROWS)], lambda c: full[1, c, pl.ds(at, ROWS)], columns, beyond
        )
    after = jnp.sum(sums[pl.ds(0, depth), :], axis=(0, 1), keepdims=True)
    beyond = jnp.sum(beyond, axis=(0, 1), keepdims=True)
    lane = lax.broadcasted_iota(jnp.int32, (1, LANES), 1)
    row = jnp.where(lane == 0, after, jnp.where(lane == 1, beyond, 0.0))
    out[...] = jnp.broadcast_to(row[None], out.shape)


def total_kernel(parts, full_low, out):
    out[...] = jnp.broadcast_to(jnp.sum(parts[...], axis=0, keepdims=True), out.shape)


def mix_kernel(cells, images, squares, plan, full, full_low, middle_high, edges_high, out, mixed, sems):
    columns, depth = full.shape[1:3]
    rows = squares.shape[0]
    seg = jnp.sqrt(squares[...].reshape(rows, LANES) / cells + EPS)
    lane = lax.broadcasted_iota(jnp.int32, (rows, LANES), 1)
    index = 2 * lax.broadcasted_iota(jnp.int32, (rows, LANES), 0) + lane
    seg = jnp.where((lane < 2) & (index < images - 1), seg, 0.0)

    def whole(values):
        return jnp.sum(values, axis=(0, 1), keepdims=True)

    total = whole(seg)
    shares = []
    for t in range(2):
        weight = (plan[t, 2] * total - whole(plan[t, 0] * seg)) / whole(plan[t, 1] * seg)
        shares.append([(1.0 - weight) * plan[t, 3 + m] + weight * plan[t, 8 + m] for m in range(5)])
    group = columns // 4
    copies = []
    for g in range(4):
        for c in range(g * group, (g + 1) * group):
            place = pl.ds(c * LANES, LANES)
            for high, row, at in (
                (edges_high, 0, 0),
                (middle_high, 0, ROWS),
                (middle_high, ROWS, 2 * ROWS),
                (edges_high, ROWS, depth - ROWS),
            ):
                high = high[c, pl.ds(row, ROWS)]
                at = pl.ds(at, ROWS)
                fields = [full_low[0, c, at], full_low[1, c, at], full[0, c, at], full[1, c, at], high]
                for t in range(2):
                    result = shares[t][0] * fields[0]
                    for m in range(1, 5):
                        result = result + shares[t][m] * fields[m]
                    mixed[t, at, place] = result
        span = pl.ds(g * group * LANES, group * LANES)
        copy = pltpu.make_async_copy(mixed.at[:, :, span], out.at[:, :, span], sems.at[g])
        copy.start()
        copies.append(copy)
    for copy in copies:
        copy.wait()


VMEM = pl.BlockSpec(memory_space=pltpu.VMEM)
SMEM = pl.BlockSpec(memory_space=pltpu.SMEM)
HBM = pl.BlockSpec(memory_space=pltpu.HBM)
ANY = pl.BlockSpec(memory_space=pl.ANY)


def call(name, kernel, shapes, ins, scratch=(), outs=VMEM, cost=0, limit=VMEM_LIMIT, aliases=None):
    return pl.pallas_call(
        kernel,
        out_shape=shapes,
        in_specs=ins,
        out_specs=jax.tree.map(lambda _: outs, shapes),
        scratch_shapes=list(scratch),
        name=name,
        input_output_aliases=aliases or {},
        cost_estimate=pl.CostEstimate(flops=cost, bytes_accessed=1 << 20, transcendentals=0),
        compiler_params=pltpu.CompilerParams(vmem_limit_bytes=limit),
    )


def body(string, tilt, source_pair):
    count, depth, width = string.shape
    columns = width // LANES
    slabs = lax.axis_size("slab")
    ranks = lax.axis_size("image")
    images = count * ranks
    half = 2 * ROWS

    def array(*shape):
        return jax.ShapeDtypeStruct(shape, jnp.float32)

    def room(*shape):
        return pltpu.VMEM(shape, jnp.float32)

    halo = array(3, ROWS, width)
    first, second = call(
        "halo", halo_kernel, (halo, halo), [HBM] * 2, [pltpu.SemaphoreType.DMA((4,))], limit=HALO_LIMIT
    )(string, tilt)
    first = lax.ppermute(first, ("image", "slab"), partners(True))
    second = lax.ppermute(second, ("image", "slab"), partners(False))
    whole = array(2, columns, depth, LANES)
    single = array(columns, half, LANES)
    full, middle, history, edge_force = call(
        "inner",
        inner_kernel,
        (whole, single, array(2, 2, columns, 3 * ROWS, LANES), array(2, columns, ROWS, LANES)),
        [VMEM] * 2,
        [room(2, columns, depth, LANES), room(2, columns, depth, LANES), room(columns, depth, LANES)],
        cost=1 << 31,
    )(string, tilt)
    middle_high = lax.ppermute(middle, "image", line("image", -1))

    def edge(name, is_second, received, full):
        return call(
            name,
            functools.partial(edge_kernel, is_second),
            (whole, single) if is_second else (whole,),
            [VMEM] * 4,
            [room(2, columns, half, LANES), room(2, columns, half, LANES), room(columns, half, LANES)],
            cost=1 << 30 if is_second else 1 << 32,
            aliases={3: 0},
        )(received, history, edge_force, full)

    (full,) = edge("edge_first", False, first, full)
    full, edges = edge("edge_second", True, second, full)
    edges_high = lax.ppermute(edges, "image", line("image", -1))
    full_low = lax.ppermute(full, "image", line("image", 1))
    sums, plan = call(
        "local",
        functools.partial(local_kernel, images),
        (array(depth + half, LANES), array(2, 13, ranks, LANES)),
        [SMEM] + [VMEM] * 2,
        cost=1 << 28,
    )(source_pair, full, middle_high)
    parts = call("square", square_kernel, array(slabs, 1, LANES), [VMEM] * 3, cost=3 << 32)(sums, full, edges_high)
    parts = lax.all_to_all(parts, "slab", 0, 0)
    squares = call("total", total_kernel, array(ranks, 1, LANES), [VMEM, ANY], cost=1 << 33)(parts, full_low)
    squares = lax.all_to_all(squares, "image", 0, 0)
    cells = depth * slabs * width
    return call(
        "mix",
        functools.partial(mix_kernel, cells, images),
        array(*string.shape),
        [VMEM] * 6,
        [room(*string.shape), pltpu.SemaphoreType.DMA((4,))],
        outs=ANY,
    )(squares, plan, full, full_low, middle_high, edges_high)


def solution(mesh):
    placed = (P("image", "slab", None), P("slab", None), P())
    return jax.shard_map(
        body, mesh=mesh, in_specs=placed, out_specs=P("image", "slab", None), check_vma=False
    )
```

```python
import functools

import jax
import jax.numpy as jnp
from jax import lax
from jax.experimental import pallas as pl
from jax.experimental.pallas import tpu as pltpu
from jax.sharding import PartitionSpec as P

SUBSTEPS = 8
DT = 0.1
EPS = 1e-06
LANES = 128
ROWS = 8
VMEM_LIMIT = 48 * 1024 * 1024
HALO_LIMIT = 54136 * 1024


def partners(axis, first):
    count = lax.axis_size(axis)
    step = -1 if first else 1
    evens = range(0, count, 2)
    return [(i, (i + step) % count) for i in evens] + [((i + step) % count, i) for i in evens]


def line(axis, distance):
    devices = range(lax.axis_size(axis))
    return [(i, i + distance) for i in devices if i + distance in devices]


def is_odd(axis):
    return lax.rem(lax.axis_index(axis), 2)


def substep(source, target, force, row, out_row, force_row, columns, keep=None, keep_row=0):
    lane = lax.broadcasted_iota(jnp.int32, (ROWS, LANES), 1)
    is_first = lane == 0
    is_last = lane == LANES - 1
    middle = [source[c % columns, pl.ds(row, ROWS), :] for c in range(-1, columns + 1)]
    right_moved = [pltpu.roll(m, 1, 1) for m in middle[:-1]]
    left_moved = [pltpu.roll(m, LANES - 1, 1) for m in middle[1:]]
    for c in range(columns):
        u = middle[c + 1]
        left = jnp.where(is_first, right_moved[c], right_moved[c + 1])
        right = jnp.where(is_last, left_moved[c + 1], left_moved[c])
        above = source[c, pl.ds(row - 1, ROWS), :]
        below = source[c, pl.ds(row + 1, ROWS), :]
        near = (above + below) + (left + right)
        result = u * (0.7 - DT * (u * u)) + (DT * near + force[c, pl.ds(force_row, ROWS), :])
        target[c, pl.ds(out_row, ROWS), :] = result
        if keep is not None:
            keep[c, pl.ds(keep_row, ROWS), :] = result


def halo_kernel(string, tilt, first, second, rows, sems):
    odd = is_odd("slab")
    last = string.shape[1] - ROWS
    columns = string.shape[2] // LANES
    copies = []
    for n, row in enumerate((odd * last, (1 - odd) * last)):
        span = pl.ds(pl.multiple_of(row, ROWS), ROWS)
        copies.append(pltpu.make_async_copy(string.at[:, span], rows.at[n, pl.ds(0, 2)], sems.at[2 * n]))
        copies.append(pltpu.make_async_copy(tilt.at[span], rows.at[n, 2], sems.at[2 * n + 1]))
    for copy in copies:
        copy.start()
    for copy in copies:
        copy.wait()
    bottom_first = jnp.full((ROWS, LANES), odd, jnp.int32) == 1
    for n, out in enumerate((first, second)):
        for c in range(columns):
            place = pl.ds(c * LANES, LANES)
            for image in range(2):
                out[pl.ds((image * columns + c) * ROWS, ROWS), :] = rows[n, image, :, place]
            whole = rows[n, 2, :, place]
            moved = pltpu.roll(whole, ROWS - 1, 0)
            near = jnp.where(bottom_first, moved, whole) if n == 0 else jnp.where(bottom_first, whole, moved)
            out[pl.ds(2 * columns * ROWS + (ROWS - 1) * c, ROWS - 1), :] = near[: ROWS - 1]


def inner_kernel(string, tilt, full, middle, history, edge_force, even, odd, force):
    depth = string.shape[1]
    columns = string.shape[2] // LANES
    bottom = 2 * SUBSTEPS - 2
    for c in range(columns):
        place = pl.ds(c * LANES, LANES)
        for image in range(2):
            rows = string[image, :, place]
            even[image, c] = rows
            history[0, image, c, pl.ds(0, ROWS), :] = rows[:ROWS]
            history[1, image, c, pl.ds(bottom, ROWS), :] = rows[depth - ROWS :]
        scaled = DT * tilt[:, place]
        force[c] = scaled
        edge_force[0, c] = scaled[:ROWS]
        edge_force[1, c] = scaled[depth - ROWS :]
    buffers = (even, odd)
    for step in range(1, SUBSTEPS + 1):
        source, target = buffers[(step - 1) % 2], buffers[step % 2]
        if step == SUBSTEPS:
            target = full
        last = depth - step - ROWS
        for image in range(2):
            for row in sorted(set(list(range(step, last, ROWS)) + [last])):
                keep, keep_row = None, 0
                if step < SUBSTEPS and row == step:
                    keep, keep_row = history.at[0, image], 2 * step
                if step < SUBSTEPS and row == last:
                    keep, keep_row = history.at[1, image], bottom - 2 * step
                substep(source.at[image], target.at[image], force, row, row, row, columns, keep, keep_row)
    middle[...] = full[0, :, pl.ds(ROWS, depth - 2 * ROWS), :]


def edge_rows(side, halo, history, edge_force, full, even, odd, force):
    columns, depth = full.shape[1:3]
    mine, theirs = ((ROWS, 0), (0, ROWS))[side]
    for c in range(columns):
        for image in range(2):
            even[image, c, pl.ds(theirs, ROWS), :] = halo[pl.ds((image * columns + c) * ROWS, ROWS), :]
        near = halo[pl.ds(2 * columns * ROWS + (ROWS - 1) * c, ROWS - 1), :]
        force[c, pl.ds(theirs + 1 - side, ROWS - 1), :] = DT * near
        force[c, pl.ds(mine, ROWS), :] = edge_force[side, c]
    buffers = (even, odd)
    for step in range(1, SUBSTEPS + 1):
        source, target = buffers[(step - 1) % 2], buffers[step % 2]
        out_row = theirs
        if step == SUBSTEPS:
            target, out_row = full, side * (depth - ROWS)
        kept = 2 * (step - 1) if side == 0 else 2 * SUBSTEPS + 4 - 2 * (step - 1)
        row, force_row = (1, step) if side == 0 else (ROWS - 1, ROWS - step)
        for image in range(2):
            for c in range(columns):
                source[image, c, pl.ds(ROWS - 2 * side, 2), :] = history[side, image, c, pl.ds(kept, 2), :]
            substep(source.at[image], target.at[image], force, row, out_row, force_row, columns)


def edge_kernel(is_second, halo, history, edge_force, inner, full, *rest):
    even, odd, force = rest[-3:]
    depth = full.shape[2]
    for side in range(2):

        @pl.when(is_odd("slab") == (1 - side if is_second else side))
        def one():
            edge_rows(side, halo, history, edge_force, full, even, odd, force)

    if is_second:
        edges = rest[0]
        edges[:, pl.ds(0, ROWS), :] = full[0, :, pl.ds(0, ROWS), :]
        edges[:, pl.ds(ROWS, ROWS), :] = full[0, :, pl.ds(depth - ROWS, ROWS), :]


def differences(upper, lower, columns, sums):
    def one(c, total):
        difference = upper(c) - lower(c)
        return total + difference * difference

    return lax.fori_loop(0, columns, one, sums, unroll=8)


def local_kernel(images, sources, full, middle_high, sums, plan):
    columns, depth = full.shape[1:3]
    inside = depth - 2 * ROWS
    zero = jnp.zeros((depth, LANES), jnp.float32)
    sums[pl.ds(0, depth), :] = differences(lambda c: full[1, c], lambda c: full[0, c], columns, zero)
    sums[pl.ds(depth, inside), :] = differences(
        lambda c: middle_high[c], lambda c: full[1, c, pl.ds(ROWS, inside)], columns, zero[:inside]
    )
    shape = plan.shape[2:]
    lane = lax.broadcasted_iota(jnp.int32, shape, 1)
    index = 2 * lax.broadcasted_iota(jnp.int32, shape, 0) + lane
    used = (lane < 2) & (index < images - 1)
    first = 2 * lax.axis_index("image")
    for t in range(2):
        target = first + t
        source = sources[target]
        place = source - (first - 2)
        plan[t, 0] = jnp.where(used & (index < source), 1.0, 0.0)
        plan[t, 1] = jnp.where(used & (index == source), 1.0, 0.0)
        plan[t, 2] = jnp.full(shape, target.astype(jnp.float32) / (images - 1))
        for m in range(5):
            plan[t, 3 + m] = jnp.full(shape, jnp.where(place == m, 1.0, 0.0))
            plan[t, 8 + m] = jnp.full(shape, jnp.where(place + 1 == m, 1.0, 0.0))


def square_kernel(sums, full, edges_high, out):
    columns, depth = full.shape[1:3]
    beyond = sums[pl.ds(depth, ROWS), :] + sums[pl.ds(depth + ROWS, ROWS), :]
    for row, at in ((0, 0), (ROWS, depth - ROWS)):
        beyond = differences(
            lambda c: edges_high[c, pl.ds(row, ROWS)], lambda c: full[1, c, pl.ds(at, ROWS)], columns, beyond
        )
    after = jnp.sum(sums[pl.ds(0, depth), :], axis=(0, 1), keepdims=True)
    beyond = jnp.sum(beyond, axis=(0, 1), keepdims=True)
    lane = lax.broadcasted_iota(jnp.int32, (1, LANES), 1)
    row = jnp.where(lane == 0, after, jnp.where(lane == 1, beyond, 0.0))
    out[...] = jnp.broadcast_to(row[None], out.shape)


def total_kernel(parts, full_low, out):
    out[...] = jnp.broadcast_to(jnp.sum(parts[...], axis=0, keepdims=True), out.shape)


def mix_kernel(cells, images, squares, plan, full, full_low, middle_high, edges_high, out, mixed, sems):
    columns, depth = full.shape[1:3]
    rows = squares.shape[0]
    seg = jnp.sqrt(squares[...].reshape(rows, LANES) / cells + EPS)
    lane = lax.broadcasted_iota(jnp.int32, (rows, LANES), 1)
    index = 2 * lax.broadcasted_iota(jnp.int32, (rows, LANES), 0) + lane
    seg = jnp.where((lane < 2) & (index < images - 1), seg, 0.0)

    def whole(values):
        return jnp.sum(values, axis=(0, 1), keepdims=True)

    total = whole(seg)
    shares = []
    for t in range(2):
        weight = (plan[t, 2] * total - whole(plan[t, 0] * seg)) / whole(plan[t, 1] * seg)
        shares.append([(1.0 - weight) * plan[t, 3 + m] + weight * plan[t, 8 + m] for m in range(5)])
    group = columns // 4
    copies = []
    for g in range(4):
        for c in range(g * group, (g + 1) * group):
            place = pl.ds(c * LANES, LANES)
            for high, row, at in (
                (edges_high, 0, 0),
                (middle_high, 0, ROWS),
                (middle_high, ROWS, 2 * ROWS),
                (edges_high, ROWS, depth - ROWS),
            ):
                high = high[c, pl.ds(row, ROWS)]
                at = pl.ds(at, ROWS)
                fields = [full_low[0, c, at], full_low[1, c, at], full[0, c, at], full[1, c, at], high]
                for t in range(2):
                    result = shares[t][0] * fields[0]
                    for m in range(1, 5):
                        result = result + shares[t][m] * fields[m]
                    mixed[t, at, place] = result
        span = pl.ds(g * group * LANES, group * LANES)
        copy = pltpu.make_async_copy(mixed.at[:, :, span], out.at[:, :, span], sems.at[g])
        copy.start()
        copies.append(copy)
    for copy in copies:
        copy.wait()


VMEM = pl.BlockSpec(memory_space=pltpu.VMEM)
SMEM = pl.BlockSpec(memory_space=pltpu.SMEM)
HBM = pl.BlockSpec(memory_space=pltpu.HBM)
ANY = pl.BlockSpec(memory_space=pl.ANY)


def call(name, kernel, shapes, ins, scratch=(), outs=VMEM, cost=0, limit=VMEM_LIMIT, aliases=None):
    return pl.pallas_call(
        kernel,
        out_shape=shapes,
        in_specs=ins,
        out_specs=jax.tree.map(lambda _: outs, shapes),
        scratch_shapes=list(scratch),
        name=name,
        input_output_aliases=aliases or {},
        cost_estimate=pl.CostEstimate(flops=cost, bytes_accessed=1 << 20, transcendentals=0),
        compiler_params=pltpu.CompilerParams(vmem_limit_bytes=limit),
    )


def body(string, tilt, source_pair):
    count, depth, width = string.shape
    columns = width // LANES
    slabs = lax.axis_size("slab")
    ranks = lax.axis_size("image")
    images = count * ranks
    half = 2 * ROWS

    def array(*shape):
        return jax.ShapeDtypeStruct(shape, jnp.float32)

    def room(*shape):
        return pltpu.VMEM(shape, jnp.float32)

    halo = array(columns * (3 * ROWS - 1), LANES)
    first, second = call(
        "halo",
        halo_kernel,
        (halo, halo),
        [HBM] * 2,
        [room(2, 3, ROWS, width), pltpu.SemaphoreType.DMA((4,))],
        limit=HALO_LIMIT,
    )(string, tilt)
    first = lax.ppermute(first, "slab", partners("slab", True))
    second = lax.ppermute(second, "slab", partners("slab", False))
    whole = array(2, columns, depth, LANES)
    single = array(columns, half, LANES)
    full, middle, history, edge_force = call(
        "inner",
        inner_kernel,
        (whole, single, array(2, 2, columns, 3 * ROWS, LANES), array(2, columns, ROWS, LANES)),
        [VMEM] * 2,
        [room(2, columns, depth, LANES), room(2, columns, depth, LANES), room(columns, depth, LANES)],
        cost=1 << 31,
    )(string, tilt)
    middle_high = lax.ppermute(middle, "image", line("image", -1))

    def edge(name, is_second, received, full):
        return call(
            name,
            functools.partial(edge_kernel, is_second),
            (whole, single) if is_second else (whole,),
            [VMEM] * 4,
            [room(2, columns, half, LANES), room(2, columns, half, LANES), room(columns, half, LANES)],
            cost=1 << 30 if is_second else 1 << 32,
            aliases={3: 0},
        )(received, history, edge_force, full)

    (full,) = edge("edge_first", False, first, full)
    full, edges = edge("edge_second", True, second, full)
    edges_high = lax.ppermute(edges, "image", line("image", -1))
    full_low = lax.ppermute(full, "image", line("image", 1))
    sums, plan = call(
        "local",
        functools.partial(local_kernel, images),
        (array(depth + half, LANES), array(2, 13, ranks, LANES)),
        [SMEM] + [VMEM] * 2,
        cost=1 << 28,
    )(source_pair, full, middle_high)
    parts = call("square", square_kernel, array(slabs, 1, LANES), [VMEM] * 3, cost=3 << 32)(sums, full, edges_high)
    parts = lax.all_to_all(parts, "slab", 0, 0)
    squares = call("total", total_kernel, array(ranks, 1, LANES), [VMEM, ANY], cost=1 << 33)(parts, full_low)
    squares = lax.all_to_all(squares, "image", 0, 0)
    cells = depth * slabs * width
    return call(
        "mix",
        functools.partial(mix_kernel, cells, images),
        array(*string.shape),
        [VMEM] * 6,
        [room(*string.shape), pltpu.SemaphoreType.DMA((4,))],
        outs=ANY,
    )(squares, plan, full, full_low, middle_high, edges_high)


def solution(mesh):
    placed = (P("image", "slab", None), P("slab", None), P())
    return jax.shard_map(
        body, mesh=mesh, in_specs=placed, out_specs=P("image", "slab", None), check_vma=False
    )
```

```python
import functools

import jax
import jax.numpy as jnp
from jax import lax
from jax.experimental import pallas as pl
from jax.experimental.pallas import tpu as pltpu
from jax.sharding import PartitionSpec as P

SUBSTEPS = 8
DT = 0.1
EPS = 1e-06
LANES = 128
ROWS = 8
VMEM_LIMIT = 48 * 1024 * 1024
HALO_LIMIT = 54136 * 1024


def partners(first):
    ranks, slabs = lax.axis_size("image"), lax.axis_size("slab")
    step = -1 if first else 1
    pairs = []
    for i in range(ranks):
        for s in range(i % 2, slabs, 2):
            here, there = i * slabs + s, i * slabs + (s + step) % slabs
            pairs += [(here, there), (there, here)]
    return pairs


def line(axis, distance):
    devices = range(lax.axis_size(axis))
    return [(i, i + distance) for i in devices if i + distance in devices]


def is_odd():
    return lax.rem(lax.axis_index("image") + lax.axis_index("slab"), 2)


def substep(source, target, force, row, out_row, force_row, columns, keep=None, keep_row=0):
    lane = lax.broadcasted_iota(jnp.int32, (ROWS, LANES), 1)
    is_first = lane == 0
    is_last = lane == LANES - 1
    middle = [source[c % columns, pl.ds(row, ROWS), :] for c in range(-1, columns + 1)]
    right_moved = [pltpu.roll(m, 1, 1) for m in middle[:-1]]
    left_moved = [pltpu.roll(m, LANES - 1, 1) for m in middle[1:]]
    for c in range(columns):
        u = middle[c + 1]
        left = jnp.where(is_first, right_moved[c], right_moved[c + 1])
        right = jnp.where(is_last, left_moved[c + 1], left_moved[c])
        above = source[c, pl.ds(row - 1, ROWS), :]
        below = source[c, pl.ds(row + 1, ROWS), :]
        near = (above + below) + (left + right)
        result = u * (0.7 - DT * (u * u)) + (DT * near + force[c, pl.ds(force_row, ROWS), :])
        target[c, pl.ds(out_row, ROWS), :] = result
        if keep is not None:
            keep[c, pl.ds(keep_row, ROWS), :] = result


def halo_kernel(string, tilt, first, second, rows, sems):
    odd = is_odd()
    last = string.shape[1] - ROWS
    columns = string.shape[2] // LANES
    copies = []
    for n, row in enumerate((odd * last, (1 - odd) * last)):
        span = pl.ds(pl.multiple_of(row, ROWS), ROWS)
        copies.append(pltpu.make_async_copy(string.at[:, span], rows.at[n, pl.ds(0, 2)], sems.at[2 * n]))
        copies.append(pltpu.make_async_copy(tilt.at[span], rows.at[n, 2], sems.at[2 * n + 1]))
    for copy in copies:
        copy.start()
    for copy in copies:
        copy.wait()
    bottom_first = jnp.full((ROWS, LANES), odd, jnp.int32) == 1
    for n, out in enumerate((first, second)):
        for c in range(columns):
            place = pl.ds(c * LANES, LANES)
            for image in range(2):
                out[pl.ds((image * columns + c) * ROWS, ROWS), :] = rows[n, image, :, place]
            whole = rows[n, 2, :, place]
            moved = pltpu.roll(whole, ROWS - 1, 0)
            near = jnp.where(bottom_first, moved, whole) if n == 0 else jnp.where(bottom_first, whole, moved)
            out[pl.ds(2 * columns * ROWS + (ROWS - 1) * c, ROWS - 1), :] = near[: ROWS - 1]


def inner_kernel(string, tilt, full, middle, history, edge_force, even, odd, force):
    depth = string.shape[1]
    columns = string.shape[2] // LANES
    bottom = 2 * SUBSTEPS - 2
    for c in range(columns):
        place = pl.ds(c * LANES, LANES)
        for image in range(2):
            rows = string[image, :, place]
            even[image, c] = rows
            history[0, image, c, pl.ds(0, ROWS), :] = rows[:ROWS]
            history[1, image, c, pl.ds(bottom, ROWS), :] = rows[depth - ROWS :]
        scaled = DT * tilt[:, place]
        force[c] = scaled
        edge_force[0, c] = scaled[:ROWS]
        edge_force[1, c] = scaled[depth - ROWS :]
    buffers = (even, odd)
    for step in range(1, SUBSTEPS + 1):
        source, target = buffers[(step - 1) % 2], buffers[step % 2]
        if step == SUBSTEPS:
            target = full
        last = depth - step - ROWS
        for image in range(2):
            for row in sorted(set(list(range(step, last, ROWS)) + [last])):
                keep, keep_row = None, 0
                if step < SUBSTEPS and row == step:
                    keep, keep_row = history.at[0, image], 2 * step
                if step < SUBSTEPS and row == last:
                    keep, keep_row = history.at[1, image], bottom - 2 * step
                substep(source.at[image], target.at[image], force, row, row, row, columns, keep, keep_row)
    middle[...] = full[0, :, pl.ds(ROWS, depth - 2 * ROWS), :]


def edge_rows(side, halo, history, edge_force, full, even, odd, force):
    columns, depth = full.shape[1:3]
    mine, theirs = ((ROWS, 0), (0, ROWS))[side]
    for c in range(columns):
        for image in range(2):
            even[image, c, pl.ds(theirs, ROWS), :] = halo[pl.ds((image * columns + c) * ROWS, ROWS), :]
        near = halo[pl.ds(2 * columns * ROWS + (ROWS - 1) * c, ROWS - 1), :]
        force[c, pl.ds(theirs + 1 - side, ROWS - 1), :] = DT * near
        force[c, pl.ds(mine, ROWS), :] = edge_force[side, c]
    buffers = (even, odd)
    for step in range(1, SUBSTEPS + 1):
        source, target = buffers[(step - 1) % 2], buffers[step % 2]
        out_row = theirs
        if step == SUBSTEPS:
            target, out_row = full, side * (depth - ROWS)
        kept = 2 * (step - 1) if side == 0 else 2 * SUBSTEPS + 4 - 2 * (step - 1)
        row, force_row = (1, step) if side == 0 else (ROWS - 1, ROWS - step)
        for image in range(2):
            for c in range(columns):
                source[image, c, pl.ds(ROWS - 2 * side, 2), :] = history[side, image, c, pl.ds(kept, 2), :]
            substep(source.at[image], target.at[image], force, row, out_row, force_row, columns)


def edge_kernel(is_second, halo, history, edge_force, inner, full, *rest):
    even, odd, force = rest[-3:]
    depth = full.shape[2]
    for side in range(2):

        @pl.when(is_odd() == (1 - side if is_second else side))
        def one():
            edge_rows(side, halo, history, edge_force, full, even, odd, force)

    if is_second:
        edges = rest[0]
        edges[:, pl.ds(0, ROWS), :] = full[0, :, pl.ds(0, ROWS), :]
        edges[:, pl.ds(ROWS, ROWS), :] = full[0, :, pl.ds(depth - ROWS, ROWS), :]


def differences(upper, lower, columns, sums):
    def one(c, total):
        difference = upper(c) - lower(c)
        return total + difference * difference

    return lax.fori_loop(0, columns, one, sums, unroll=8)


def local_kernel(images, sources, full, middle_high, sums, plan):
    columns, depth = full.shape[1:3]
    inside = depth - 2 * ROWS
    zero = jnp.zeros((depth, LANES), jnp.float32)
    sums[pl.ds(0, depth), :] = differences(lambda c: full[1, c], lambda c: full[0, c], columns, zero)
    sums[pl.ds(depth, inside), :] = differences(
        lambda c: middle_high[c], lambda c: full[1, c, pl.ds(ROWS, inside)], columns, zero[:inside]
    )
    shape = plan.shape[2:]
    lane = lax.broadcasted_iota(jnp.int32, shape, 1)
    index = 2 * lax.broadcasted_iota(jnp.int32, shape, 0) + lane
    used = (lane < 2) & (index < images - 1)
    first = 2 * lax.axis_index("image")
    for t in range(2):
        target = first + t
        source = sources[target]
        place = source - (first - 2)
        plan[t, 0] = jnp.where(used & (index < source), 1.0, 0.0)
        plan[t, 1] = jnp.where(used & (index == source), 1.0, 0.0)
        plan[t, 2] = jnp.full(shape, target.astype(jnp.float32) / (images - 1))
        for m in range(5):
            plan[t, 3 + m] = jnp.full(shape, jnp.where(place == m, 1.0, 0.0))
            plan[t, 8 + m] = jnp.full(shape, jnp.where(place + 1 == m, 1.0, 0.0))


def square_kernel(sums, full, edges_high, out):
    columns, depth = full.shape[1:3]
    beyond = sums[pl.ds(depth, ROWS), :] + sums[pl.ds(depth + ROWS, ROWS), :]
    for row, at in ((0, 0), (ROWS, depth - ROWS)):
        beyond = differences(
            lambda c: edges_high[c, pl.ds(row, ROWS)], lambda c: full[1, c, pl.ds(at, ROWS)], columns, beyond
        )
    after = jnp.sum(sums[pl.ds(0, depth), :], axis=(0, 1), keepdims=True)
    beyond = jnp.sum(beyond, axis=(0, 1), keepdims=True)
    lane = lax.broadcasted_iota(jnp.int32, (1, LANES), 1)
    row = jnp.where(lane == 0, after, jnp.where(lane == 1, beyond, 0.0))
    out[...] = jnp.broadcast_to(row[None], out.shape)


def total_kernel(parts, full_low, out):
    out[...] = jnp.broadcast_to(jnp.sum(parts[...], axis=0, keepdims=True), out.shape)


def mix_kernel(cells, images, squares, plan, full, full_low, middle_high, edges_high, out, mixed, sems):
    columns, depth = full.shape[1:3]
    rows = squares.shape[0]
    seg = jnp.sqrt(squares[...].reshape(rows, LANES) / cells + EPS)
    lane = lax.broadcasted_iota(jnp.int32, (rows, LANES), 1)
    index = 2 * lax.broadcasted_iota(jnp.int32, (rows, LANES), 0) + lane
    seg = jnp.where((lane < 2) & (index < images - 1), seg, 0.0)

    def whole(values):
        return jnp.sum(values, axis=(0, 1), keepdims=True)

    total = whole(seg)
    shares = []
    for t in range(2):
        weight = (plan[t, 2] * total - whole(plan[t, 0] * seg)) / whole(plan[t, 1] * seg)
        shares.append([(1.0 - weight) * plan[t, 3 + m] + weight * plan[t, 8 + m] for m in range(5)])
    group = columns // 4
    copies = []
    for g in range(4):
        for c in range(g * group, (g + 1) * group):
            place = pl.ds(c * LANES, LANES)
            for high, row, at in (
                (edges_high, 0, 0),
                (middle_high, 0, ROWS),
                (middle_high, ROWS, 2 * ROWS),
                (edges_high, ROWS, depth - ROWS),
            ):
                high = high[c, pl.ds(row, ROWS)]
                at = pl.ds(at, ROWS)
                fields = [full_low[0, c, at], full_low[1, c, at], full[0, c, at], full[1, c, at], high]
                for t in range(2):
                    result = shares[t][0] * fields[0]
                    for m in range(1, 5):
                        result = result + shares[t][m] * fields[m]
                    mixed[t, at, place] = result
        span = pl.ds(g * group * LANES, group * LANES)
        copy = pltpu.make_async_copy(mixed.at[:, :, span], out.at[:, :, span], sems.at[g])
        copy.start()
        copies.append(copy)
    for copy in copies:
        copy.wait()


VMEM = pl.BlockSpec(memory_space=pltpu.VMEM)
SMEM = pl.BlockSpec(memory_space=pltpu.SMEM)
HBM = pl.BlockSpec(memory_space=pltpu.HBM)
ANY = pl.BlockSpec(memory_space=pl.ANY)


def call(name, kernel, shapes, ins, scratch=(), outs=VMEM, cost=0, limit=VMEM_LIMIT, aliases=None):
    return pl.pallas_call(
        kernel,
        out_shape=shapes,
        in_specs=ins,
        out_specs=jax.tree.map(lambda _: outs, shapes),
        scratch_shapes=list(scratch),
        name=name,
        input_output_aliases=aliases or {},
        cost_estimate=pl.CostEstimate(flops=cost, bytes_accessed=1 << 20, transcendentals=0),
        compiler_params=pltpu.CompilerParams(vmem_limit_bytes=limit),
    )


def body(string, tilt, source_pair):
    count, depth, width = string.shape
    columns = width // LANES
    slabs = lax.axis_size("slab")
    ranks = lax.axis_size("image")
    images = count * ranks
    half = 2 * ROWS

    def array(*shape):
        return jax.ShapeDtypeStruct(shape, jnp.float32)

    def room(*shape):
        return pltpu.VMEM(shape, jnp.float32)

    halo = array(columns * (3 * ROWS - 1), LANES)
    first, second = call(
        "halo",
        halo_kernel,
        (halo, halo),
        [HBM] * 2,
        [room(2, 3, ROWS, width), pltpu.SemaphoreType.DMA((4,))],
        limit=HALO_LIMIT,
    )(string, tilt)
    first = lax.ppermute(first, ("image", "slab"), partners(True))
    second = lax.ppermute(second, ("image", "slab"), partners(False))
    whole = array(2, columns, depth, LANES)
    single = array(columns, half, LANES)
    full, middle, history, edge_force = call(
        "inner",
        inner_kernel,
        (whole, single, array(2, 2, columns, 3 * ROWS, LANES), array(2, columns, ROWS, LANES)),
        [VMEM] * 2,
        [room(2, columns, depth, LANES), room(2, columns, depth, LANES), room(columns, depth, LANES)],
        cost=1 << 31,
    )(string, tilt)
    middle_high = lax.ppermute(middle, "image", line("image", -1))

    def edge(name, is_second, received, full):
        return call(
            name,
            functools.partial(edge_kernel, is_second),
            (whole, single) if is_second else (whole,),
            [VMEM] * 4,
            [room(2, columns, half, LANES), room(2, columns, half, LANES), room(columns, half, LANES)],
            cost=1 << 30 if is_second else 1 << 32,
            aliases={3: 0},
        )(received, history, edge_force, full)

    (full,) = edge("edge_first", False, first, full)
    full, edges = edge("edge_second", True, second, full)
    edges_high = lax.ppermute(edges, "image", line("image", -1))
    full_low = lax.ppermute(full, "image", line("image", 1))
    sums, plan = call(
        "local",
        functools.partial(local_kernel, images),
        (array(depth + half, LANES), array(2, 13, ranks, LANES)),
        [SMEM] + [VMEM] * 2,
        cost=1 << 28,
    )(source_pair, full, middle_high)
    parts = call("square", square_kernel, array(slabs, 1, LANES), [VMEM] * 3, cost=3 << 32)(sums, full, edges_high)
    parts = lax.all_to_all(parts, "slab", 0, 0)
    squares = call("total", total_kernel, array(ranks, 1, LANES), [VMEM, ANY], cost=1 << 33)(parts, full_low)
    squares = lax.all_to_all(squares, "image", 0, 0)
    cells = depth * slabs * width
    return call(
        "mix",
        functools.partial(mix_kernel, cells, images),
        array(*string.shape),
        [VMEM] * 6,
        [room(*string.shape), pltpu.SemaphoreType.DMA((4,))],
        outs=ANY,
    )(squares, plan, full, full_low, middle_high, edges_high)


def solution(mesh):
    placed = (P("image", "slab", None), P("slab", None), P())
    return jax.shard_map(
        body, mesh=mesh, in_specs=placed, out_specs=P("image", "slab", None), check_vma=False
    )
```

```python
import functools

import jax
import jax.numpy as jnp
from jax import lax
from jax.experimental import pallas as pl
from jax.experimental.pallas import tpu as pltpu
from jax.sharding import PartitionSpec as P

SUBSTEPS = 8
DT = 0.1
EPS = 1e-06
LANES = 128
ROWS = 8
VMEM_LIMIT = 48 * 1024 * 1024
HALO_LIMIT = 54136 * 1024


def partners(first):
    ranks, slabs = lax.axis_size("image"), lax.axis_size("slab")
    step = -1 if first else 1
    pairs = []
    for i in range(ranks):
        for s in range(i % 2, slabs, 2):
            here, there = i * slabs + s, i * slabs + (s + step) % slabs
            pairs += [(here, there), (there, here)]
    return pairs


def line(axis, distance):
    devices = range(lax.axis_size(axis))
    return [(i, i + distance) for i in devices if i + distance in devices]


def is_odd():
    return lax.rem(lax.axis_index("image") + lax.axis_index("slab"), 2)


def substep(source, target, force, row, out_row, force_row, columns, keep=None, keep_row=0):
    lane = lax.broadcasted_iota(jnp.int32, (ROWS, LANES), 1)
    is_first = lane == 0
    is_last = lane == LANES - 1
    middle = [source[c % columns, pl.ds(row, ROWS), :] for c in range(-1, columns + 1)]
    right_moved = [pltpu.roll(m, 1, 1) for m in middle[:-1]]
    left_moved = [pltpu.roll(m, LANES - 1, 1) for m in middle[1:]]
    for c in range(columns):
        u = middle[c + 1]
        left = jnp.where(is_first, right_moved[c], right_moved[c + 1])
        right = jnp.where(is_last, left_moved[c + 1], left_moved[c])
        above = source[c, pl.ds(row - 1, ROWS), :]
        below = source[c, pl.ds(row + 1, ROWS), :]
        near = (above + below) + (left + right)
        result = u * (0.7 - DT * (u * u)) + (DT * near + force[c, pl.ds(force_row, ROWS), :])
        target[c, pl.ds(out_row, ROWS), :] = result
        if keep is not None:
            keep[c, pl.ds(keep_row, ROWS), :] = result


def halo_kernel(string, tilt, first, second, rows, sems):
    odd = is_odd()
    last = string.shape[1] - ROWS
    columns = string.shape[2] // LANES
    copies = []
    for n, row in enumerate((odd * last, (1 - odd) * last)):
        span = pl.ds(pl.multiple_of(row, ROWS), ROWS)
        copies.append(pltpu.make_async_copy(string.at[:, span], rows.at[n, pl.ds(0, 2)], sems.at[2 * n]))
        copies.append(pltpu.make_async_copy(tilt.at[span], rows.at[n, 2], sems.at[2 * n + 1]))
    for copy in copies:
        copy.start()
    for copy in copies:
        copy.wait()
    bottom_first = jnp.full((ROWS, LANES), odd, jnp.int32) == 1
    for n, out in enumerate((first, second)):
        for c in range(columns):
            place = pl.ds(c * LANES, LANES)
            for image in range(2):
                out[pl.ds((image * columns + c) * ROWS, ROWS), :] = rows[n, image, :, place]
            whole = rows[n, 2, :, place]
            moved = pltpu.roll(whole, ROWS - 1, 0)
            near = jnp.where(bottom_first, moved, whole) if n == 0 else jnp.where(bottom_first, whole, moved)
            out[pl.ds(2 * columns * ROWS + (ROWS - 1) * c, ROWS - 1), :] = near[: ROWS - 1]


def inner_kernel(string, tilt, full, middle, history, edge_force, even, odd, force):
    depth = string.shape[1]
    columns = string.shape[2] // LANES
    bottom = 2 * SUBSTEPS - 2
    for c in range(columns):
        place = pl.ds(c * LANES, LANES)
        for image in range(2):
            rows = string[image, :, place]
            even[image, c] = rows
            history[0, image, c, pl.ds(0, ROWS), :] = rows[:ROWS]
            history[1, image, c, pl.ds(bottom, ROWS), :] = rows[depth - ROWS :]
        scaled = DT * tilt[:, place]
        force[c] = scaled
        edge_force[0, c] = scaled[:ROWS]
        edge_force[1, c] = scaled[depth - ROWS :]
    buffers = (even, odd)
    for step in range(1, SUBSTEPS + 1):
        source, target = buffers[(step - 1) % 2], buffers[step % 2]
        if step == SUBSTEPS:
            target = full
        last = depth - step - ROWS
        for image in range(2):
            for row in sorted(set(list(range(step, last, ROWS)) + [last])):
                keep, keep_row = None, 0
                if step < SUBSTEPS and row == step:
                    keep, keep_row = history.at[0, image], 2 * step
                if step < SUBSTEPS and row == last:
                    keep, keep_row = history.at[1, image], bottom - 2 * step
                substep(source.at[image], target.at[image], force, row, row, row, columns, keep, keep_row)
    middle[...] = full[0, :, pl.ds(ROWS, depth - 2 * ROWS), :]


def edge_kernel(first, second, history, edge_force, inner, full, edges, even, odd, force):
    columns, depth = full.shape[1:3]
    tall = jnp.full((ROWS, LANES), is_odd(), jnp.int32) == 1

    def received(side, span, rows):
        pair = (first[span, :], second[span, :])
        return jnp.where(tall[:rows], pair[1 - side], pair[side])

    for side in range(2):
        mine, theirs = ((ROWS, 0), (0, ROWS))[side]
        for c in range(columns):
            for image in range(2):
                span = pl.ds((image * columns + c) * ROWS, ROWS)
                even[side, image, c, pl.ds(theirs, ROWS), :] = received(side, span, ROWS)
            near = received(side, pl.ds(2 * columns * ROWS + (ROWS - 1) * c, ROWS - 1), ROWS - 1)
            force[side, c, pl.ds(theirs + 1 - side, ROWS - 1), :] = DT * near
            force[side, c, pl.ds(mine, ROWS), :] = edge_force[side, c]
    buffers = (even, odd)
    for step in range(1, SUBSTEPS + 1):
        source, target = buffers[(step - 1) % 2], buffers[step % 2]
        for image in range(2):
            for side in range(2):
                out, out_row = target.at[side, image], (0, ROWS)[side]
                if step == SUBSTEPS:
                    out, out_row = full.at[image], side * (depth - ROWS)
                kept = 2 * (step - 1) if side == 0 else 2 * SUBSTEPS + 4 - 2 * (step - 1)
                row, force_row = (1, step) if side == 0 else (ROWS - 1, ROWS - step)
                for c in range(columns):
                    source[side, image, c, pl.ds(ROWS - 2 * side, 2), :] = history[side, image, c, pl.ds(kept, 2), :]
                substep(source.at[side, image], out, force.at[side], row, out_row, force_row, columns)
    edges[:, pl.ds(0, ROWS), :] = full[0, :, pl.ds(0, ROWS), :]
    edges[:, pl.ds(ROWS, ROWS), :] = full[0, :, pl.ds(depth - ROWS, ROWS), :]


def differences(upper, lower, columns, sums):
    def one(c, total):
        difference = upper(c) - lower(c)
        return total + difference * difference

    return lax.fori_loop(0, columns, one, sums, unroll=8)


def local_kernel(images, sources, full, middle_high, sums, plan):
    columns, depth = full.shape[1:3]
    inside = depth - 2 * ROWS
    zero = jnp.zeros((depth, LANES), jnp.float32)
    sums[pl.ds(0, depth), :] = differences(lambda c: full[1, c], lambda c: full[0, c], columns, zero)
    sums[pl.ds(depth, inside), :] = differences(
        lambda c: middle_high[c], lambda c: full[1, c, pl.ds(ROWS, inside)], columns, zero[:inside]
    )
    shape = plan.shape[2:]
    lane = lax.broadcasted_iota(jnp.int32, shape, 1)
    index = 2 * lax.broadcasted_iota(jnp.int32, shape, 0) + lane
    used = (lane < 2) & (index < images - 1)
    first = 2 * lax.axis_index("image")
    for t in range(2):
        target = first + t
        source = sources[target]
        place = source - (first - 2)
        plan[t, 0] = jnp.where(used & (index < source), 1.0, 0.0)
        plan[t, 1] = jnp.where(used & (index == source), 1.0, 0.0)
        plan[t, 2] = jnp.full(shape, target.astype(jnp.float32) / (images - 1))
        for m in range(5):
            plan[t, 3 + m] = jnp.full(shape, jnp.where(place == m, 1.0, 0.0))
            plan[t, 8 + m] = jnp.full(shape, jnp.where(place + 1 == m, 1.0, 0.0))


def square_kernel(sums, full, edges_high, out):
    columns, depth = full.shape[1:3]
    beyond = sums[pl.ds(depth, ROWS), :] + sums[pl.ds(depth + ROWS, ROWS), :]
    for row, at in ((0, 0), (ROWS, depth - ROWS)):
        beyond = differences(
            lambda c: edges_high[c, pl.ds(row, ROWS)], lambda c: full[1, c, pl.ds(at, ROWS)], columns, beyond
        )
    after = jnp.sum(sums[pl.ds(0, depth), :], axis=(0, 1), keepdims=True)
    beyond = jnp.sum(beyond, axis=(0, 1), keepdims=True)
    lane = lax.broadcasted_iota(jnp.int32, (1, LANES), 1)
    row = jnp.where(lane == 0, after, jnp.where(lane == 1, beyond, 0.0))
    out[...] = jnp.broadcast_to(row[None], out.shape)


def total_kernel(parts, full_low, out):
    out[...] = jnp.broadcast_to(jnp.sum(parts[...], axis=0, keepdims=True), out.shape)


def mix_kernel(cells, images, squares, plan, full, full_low, middle_high, edges_high, out, mixed, sems):
    columns, depth = full.shape[1:3]
    rows = squares.shape[0]
    seg = jnp.sqrt(squares[...].reshape(rows, LANES) / cells + EPS)
    lane = lax.broadcasted_iota(jnp.int32, (rows, LANES), 1)
    index = 2 * lax.broadcasted_iota(jnp.int32, (rows, LANES), 0) + lane
    seg = jnp.where((lane < 2) & (index < images - 1), seg, 0.0)

    def whole(values):
        return jnp.sum(values, axis=(0, 1), keepdims=True)

    total = whole(seg)
    shares = []
    for t in range(2):
        weight = (plan[t, 2] * total - whole(plan[t, 0] * seg)) / whole(plan[t, 1] * seg)
        shares.append([(1.0 - weight) * plan[t, 3 + m] + weight * plan[t, 8 + m] for m in range(5)])
    group = columns // 4
    copies = []
    for g in range(4):
        for c in range(g * group, (g + 1) * group):
            place = pl.ds(c * LANES, LANES)
            for high, row, at in (
                (edges_high, 0, 0),
                (middle_high, 0, ROWS),
                (middle_high, ROWS, 2 * ROWS),
                (edges_high, ROWS, depth - ROWS),
            ):
                high = high[c, pl.ds(row, ROWS)]
                at = pl.ds(at, ROWS)
                fields = [full_low[0, c, at], full_low[1, c, at], full[0, c, at], full[1, c, at], high]
                for t in range(2):
                    result = shares[t][0] * fields[0]
                    for m in range(1, 5):
                        result = result + shares[t][m] * fields[m]
                    mixed[t, at, place] = result
        span = pl.ds(g * group * LANES, group * LANES)
        copy = pltpu.make_async_copy(mixed.at[:, :, span], out.at[:, :, span], sems.at[g])
        copy.start()
        copies.append(copy)
    for copy in copies:
        copy.wait()


VMEM = pl.BlockSpec(memory_space=pltpu.VMEM)
SMEM = pl.BlockSpec(memory_space=pltpu.SMEM)
HBM = pl.BlockSpec(memory_space=pltpu.HBM)
ANY = pl.BlockSpec(memory_space=pl.ANY)


def call(name, kernel, shapes, ins, scratch=(), outs=VMEM, cost=0, limit=VMEM_LIMIT, aliases=None):
    return pl.pallas_call(
        kernel,
        out_shape=shapes,
        in_specs=ins,
        out_specs=jax.tree.map(lambda _: outs, shapes),
        scratch_shapes=list(scratch),
        name=name,
        input_output_aliases=aliases or {},
        cost_estimate=pl.CostEstimate(flops=cost, bytes_accessed=1 << 20, transcendentals=0),
        compiler_params=pltpu.CompilerParams(vmem_limit_bytes=limit),
    )


def body(string, tilt, source_pair):
    count, depth, width = string.shape
    columns = width // LANES
    slabs = lax.axis_size("slab")
    ranks = lax.axis_size("image")
    images = count * ranks
    half = 2 * ROWS

    def array(*shape):
        return jax.ShapeDtypeStruct(shape, jnp.float32)

    def room(*shape):
        return pltpu.VMEM(shape, jnp.float32)

    halo = array(columns * (3 * ROWS - 1), LANES)
    first, second = call(
        "halo",
        halo_kernel,
        (halo, halo),
        [HBM] * 2,
        [room(2, 3, ROWS, width), pltpu.SemaphoreType.DMA((4,))],
        limit=HALO_LIMIT,
    )(string, tilt)
    first = lax.ppermute(first, ("image", "slab"), partners(True))
    second = lax.ppermute(second, ("image", "slab"), partners(False))
    whole = array(2, columns, depth, LANES)
    single = array(columns, half, LANES)
    full, middle, history, edge_force = call(
        "inner",
        inner_kernel,
        (whole, single, array(2, 2, columns, 3 * ROWS, LANES), array(2, columns, ROWS, LANES)),
        [VMEM] * 2,
        [room(2, columns, depth, LANES), room(2, columns, depth, LANES), room(columns, depth, LANES)],
        cost=1 << 31,
    )(string, tilt)
    middle_high = lax.ppermute(middle, "image", line("image", -1))

    full, edges = call(
        "edge",
        edge_kernel,
        (whole, single),
        [VMEM] * 5,
        [room(2, 2, columns, half, LANES), room(2, 2, columns, half, LANES), room(2, columns, half, LANES)],
        cost=1 << 31,
        aliases={4: 0},
    )(first, second, history, edge_force, full)
    edges_high = lax.ppermute(edges, "image", line("image", -1))
    full_low = lax.ppermute(full, "image", line("image", 1))
    sums, plan = call(
        "local",
        functools.partial(local_kernel, images),
        (array(depth + half, LANES), array(2, 13, ranks, LANES)),
        [SMEM] + [VMEM] * 2,
        cost=1 << 28,
    )(source_pair, full, middle_high)
    parts = call("square", square_kernel, array(slabs, 1, LANES), [VMEM] * 3, cost=3 << 32)(sums, full, edges_high)
    parts = lax.all_to_all(parts, "slab", 0, 0)
    squares = call("total", total_kernel, array(ranks, 1, LANES), [VMEM, ANY], cost=1 << 33)(parts, full_low)
    squares = lax.all_to_all(squares, "image", 0, 0)
    cells = depth * slabs * width
    return call(
        "mix",
        functools.partial(mix_kernel, cells, images),
        array(*string.shape),
        [VMEM] * 6,
        [room(*string.shape), pltpu.SemaphoreType.DMA((4,))],
        outs=ANY,
    )(squares, plan, full, full_low, middle_high, edges_high)


def solution(mesh):
    placed = (P("image", "slab", None), P("slab", None), P())
    return jax.shard_map(
        body, mesh=mesh, in_specs=placed, out_specs=P("image", "slab", None), check_vma=False
    )
```
